256 devices in a mesh: island: 8 (over z_hi, x), fsdp: 32 (over y, z_lo, core).
Axes of the slice: x: 4, y: 4, z: 8 (z_hi: 2, z_lo: 4; z = z_hi * 4 + z_lo), core: 2. Of those that a mesh axis runs over, the one named last changes fastest.
Arguments:
- current: bfloat16 [8, 4, 8192, 512], P('island', None, 'fsdp'), may hold values from -6 to 6
- anchor: bfloat16 [4, 8192, 512], P(None, 'fsdp'), may hold values from -6 to 6
- momentum: float32 [4, 8192, 512], P(None, 'fsdp'), may hold values from -4 to 4
- tokens: bfloat16 [131072, 8192], P(('island', 'fsdp')), may hold values from -6 to 6
- fragment: int32 [1], replicated, may hold values from 0 to 3
Outputs:
- new_current: bfloat16 [8, 4, 8192, 512], P('island', None, 'fsdp')
- new_momentum: float32 [4, 8192, 512], P(None, 'fsdp')
- keys: bfloat16 [131072, 512], P(('island', 'fsdp'))
The draws below stay inside these ranges and needn't reach their ends.
All inputs are finite; a program needn't handle non-finite values.
Results may differ from the reference program's by a relative error of at most 0.0049.
Values may be sent and summed in bfloat16 or wider, within the bound.
A program may use at most 64 MiB of HBM per device.

```python
import math
import jax
import jax.numpy as jnp
from jax import lax

D = 8192
KV_HEADS = 4
HEAD_DIM = 128
FRAGS = 4
TOKENS = 131072
N_ISLAND = 8


def levels(key, dims, shards, smallest, top_value):
    def one(axis_at, blocks):
        draws = jax.random.uniform(jax.random.fold_in(jax.random.fold_in(key, 6), axis_at), (blocks,), jnp.float32, smallest / len(shards), top_value / len(shards))
        return jnp.repeat(jnp.exp(draws), dims[axis_at] // blocks).reshape((-1,) + (1,) * (len(dims) - axis_at - 1))

    loudness = one(*shards[0])
    for cut in shards[1:]:
        loudness = loudness * one(*cut)
    return loudness


def centred(rng, dims, width, most, cuts=(), kind=jnp.bfloat16):
    values = jax.random.normal(rng, dims, jnp.float32) * width
    if len(cuts) > 0:
        values = levels(rng, dims, cuts, -0.22, 0.18) * values
    return jnp.clip(values, min=-most, max=most).astype(kind)


def setup_inputs(seed: int = 0) -> dict:
    arg_keys = jax.random.split(jax.random.key(seed), 6)
    current = centred(arg_keys[0], (N_ISLAND, FRAGS, D, KV_HEADS * HEAD_DIM), 1.0, 6.0, ((0, 8), (2, 32)))
    anchor = centred(arg_keys[1], (FRAGS, D, KV_HEADS * HEAD_DIM), 1.0, 6.0, ((1, 32),))
    momentum = centred(arg_keys[2], (FRAGS, D, KV_HEADS * HEAD_DIM), 0.5, 4.0, ((1, 32),), jnp.float32)
    tokens = centred(arg_keys[3], (TOKENS, D), 1.0, 6.0, ((0, 256),))
    fragment = jax.random.randint(arg_keys[4], (1,), 0, FRAGS).astype(jnp.int32)
    return {"current": current, "anchor": anchor, "momentum": momentum, "tokens": tokens, "fragment": fragment}


outer_momentum = 0.9
outer_rate = 0.7
blend_local = 0.5

def project_island(pair):
    return jnp.dot(pair[0], pair[1], preferred_element_type=jnp.float32)

def reference(current, anchor, momentum, tokens, fragment):
    slot_index = fragment[0].astype(jnp.int32)
    cur_layer = lax.dynamic_index_in_dim(current, slot_index, 1, keepdims=False).astype(jnp.float32)
    anc_layer = lax.dynamic_index_in_dim(anchor, slot_index, 0, keepdims=False).astype(jnp.float32)
    mom_layer = lax.dynamic_index_in_dim(momentum, slot_index, 0, keepdims=False)
    drift_mean = lax.optimization_barrier(jnp.sum(cur_layer - anc_layer[None], axis=0)) / N_ISLAND
    mom_next = outer_momentum * mom_layer + drift_mean
    global_new = anc_layer + outer_rate * (outer_momentum * mom_next + drift_mean)
    blended = (blend_local * cur_layer + (1.0 - blend_local) * global_new[None]).astype(jnp.bfloat16)
    new_current = lax.dynamic_update_index_in_dim(current, blended, slot_index, 1)
    new_momentum = lax.dynamic_update_index_in_dim(momentum, mom_next, slot_index, 0)
    grouped = tokens.reshape(N_ISLAND, -1, D)
    products = lax.map(project_island, (grouped, blended))
    keys = (products * (1.0 / math.sqrt(D))).reshape(-1, KV_HEADS * HEAD_DIM).astype(jnp.bfloat16)
    return (new_current, new_momentum, keys)
```

```python
import math

import jax
import jax.numpy as jnp
from jax import lax
from jax.experimental import pallas as pl
from jax.experimental.pallas import tpu as pltpu
from jax.sharding import PartitionSpec as P

D = 8192
WIDTH = 512
ROWS = 256
G = 16
CHUNKS = 4
MESH = pl.DeviceIdType.MESH

outer_momentum = 0.9
outer_rate = 0.7
blend_local = 0.5

PIECES = ((0, 4), (4, 4), (8, 5), (13, 3))
PARTS = (((0, 2), (2, 2)), ((4, 2), (6, 2)), ((8, 3), (11, 2)), ((13, 1), (14, 2)))
YP = 3
ZROWS = 13 * G
YROWS = 3 * G
PLUS = [sum(PARTS[p][0][1] for p in range(3)) * G, PARTS[YP][0][1] * G]
MINUS = [sum(PARTS[p][1][1] for p in range(3)) * G, PARTS[YP][1][1] * G]


def kernel(frag, cur_hbm, anc_hbm, mom_hbm, tok_hbm,
           keys, blend_hbm, momn_hbm,
           cur4, anc4, mom4, tok, w, cur, raw, s_out, s_in, drift, momn, acc,
           load_sem, out_sem, raw_ss, raw_rs, s_ss, s_rs, d_ss, d_rs,
           g_ss, g_rs, sib_ss, sib_rs):
    island = lax.axis_index("island")
    fsdp = lax.axis_index("fsdp")
    zh, x = island // 4, island % 4
    y, z, c = fsdp // 8, (fsdp // 2) % 4, fsdp % 2

    def at(zh_, x_, y_, z_, c_):
        return (zh_ * 4 + x_, y_ * 8 + z_ * 2 + c_)

    y_up, y_dn, y_far = (y + 1) % 4, (y + 3) % 4, (y + 2) % 4
    has_up, has_dn = z < 3, z > 0
    z_up, z_dn = jnp.minimum(z + 1, 3), jnp.maximum(z - 1, 0)
    dev_yu, dev_yd = at(zh, x, y_up, z, c), at(zh, x, y_dn, z, c)
    dev_zu, dev_zd = at(zh, x, y, z_up, c), at(zh, x, y, z_dn, c)
    dev_sib = at(zh, x, y, z, 1 - c)
    dev_far = at(1 - zh, x, y, z, c)
    dev_x = [at(zh, (x + d) % 4, y, z, c) for d in (1, 2, 3)]

    loads = [
        pltpu.make_async_copy(cur_hbm.at[0], cur4, load_sem.at[0]),
        pltpu.make_async_copy(anc_hbm, anc4, load_sem.at[1]),
        pltpu.make_async_copy(mom_hbm, mom4, load_sem.at[2]),
        pltpu.make_async_copy(tok_hbm, tok, load_sem.at[3]),
    ]
    for load in loads:
        load.start()

    barrier = pltpu.get_barrier_semaphore()
    for dev in (*dev_x, dev_far, dev_yu, dev_yd, dev_sib):
        pl.semaphore_signal(barrier, inc=1, device_id=dev, device_id_type=MESH)

    @pl.when(has_up)
    def _():
        pl.semaphore_signal(barrier, inc=1, device_id=dev_zu, device_id_type=MESH)

    @pl.when(has_dn)
    def _():
        pl.semaphore_signal(barrier, inc=1, device_id=dev_zd, device_id_type=MESH)

    ends = jnp.where(has_up, 1, 0) + jnp.where(has_dn, 1, 0)

    fr = frag[0]
    loads[0].wait()
    cur[...] = cur4[fr].reshape(16, G, WIDTH)
    pl.semaphore_wait(barrier, 7 + ends)

    def remote(src, dst, ss, rs, dev):
        return pltpu.make_async_remote_copy(
            src_ref=src, dst_ref=dst, send_sem=ss, recv_sem=rs,
            device_id=dev, device_id_type=MESH,
        )

    def raw_copy(k, d):
        to = (x + d + 1) % 4
        return remote(cur.at[4 * k + to], raw.at[d, k], raw_ss.at[d, k], raw_rs.at[d, k], dev_x[d])

    def s_copy(k):
        return remote(s_out.at[k], s_in.at[k], s_ss.at[k], s_rs.at[k], dev_far)

    def d_copy(k, d):
        mine = 4 * k + x
        return remote(drift.at[mine], drift.at[mine], d_ss.at[d, k], d_rs.at[d, k], dev_x[d])

    def d_wait(k, d):
        theirs = 4 * k + (x + 3 - d) % 4
        remote(drift.at[theirs], drift.at[theirs], d_ss.at[d, k], d_rs.at[d, k], dev_x[d]).wait_recv()

    for k in range(CHUNKS):
        for d in range(3):
            raw_copy(k, d).start()
    acc[...] = jnp.zeros_like(acc)
    loads[1].wait()
    for k in range(CHUNKS):
        for d in range(3):
            raw_copy(k, d).wait_recv()
        mine = 4 * k + x
        anc = anc4[fr, pl.ds(pl.multiple_of(mine * G, G), G), :].astype(jnp.float32)
        total = cur[mine].astype(jnp.float32) - anc
        for d in range(3):
            total += raw[d, k].astype(jnp.float32) - anc
        s_out[k] = total.astype(jnp.bfloat16)
        s_copy(k).start()

    def exchange(k):
        s_copy(k).wait_recv()
        both = s_out[k].astype(jnp.float32) + s_in[k].astype(jnp.float32)
        drift[4 * k + x] = (both * 0.125).astype(jnp.bfloat16)
        for d in range(3):
            d_copy(k, d).start()

    def block(oy, oz, first, count):
        return w.at[oy * 8 + oz * 2 + c, pl.ds(first, count)]

    def go(t, dev, oy, oz, p, h, span):
        ref = block(oy, oz, *span)
        return remote(ref, ref, g_ss.at[t], g_rs.at[oy * 4 + oz, p, h], dev)

    def arrive(oy, oz, p, h, span):
        go(0, dev_yu, oy, oz, p, h, span).wait_recv()

    def to_y(oy, oz, p):
        go(0, dev_yu, oy, oz, p, 0, PIECES[p]).start()
        go(1, dev_yd, oy, oz, p, 0, PIECES[p]).start()

    def to_z(oy, oz, p, up, dn):
        if up is not None:
            @pl.when(up)
            def _():
                go(2, dev_zu, oy, oz, p, 0, PIECES[p]).start()
        if dn is not None:
            @pl.when(dn)
            def _():
                go(3, dev_zd, oy, oz, p, 0, PIECES[p]).start()

    def sib(oy, oz, half):
        ref = block(oy, oz, 8 * half, 8)
        return remote(ref, ref, sib_ss.at[0], sib_rs.at[oy * 4 + oz, half], dev_sib)

    def sib_wait(oy, oz, half):
        ref = w.at[oy * 8 + oz * 2 + 1 - c, pl.ds(8 * half, 8)]
        remote(ref, ref, sib_ss.at[0], sib_rs.at[oy * 4 + oz, half], dev_sib).wait_recv()

    outs = [
        pltpu.make_async_copy(w.at[fsdp], blend_hbm, out_sem.at[0]),
        pltpu.make_async_copy(momn, momn_hbm, out_sem.at[1]),
    ]

    def own(k):
        for d in range(3):
            d_wait(k, d)
        rows = pl.ds(64 * k, 64)
        anc = anc4[fr, rows, :].astype(jnp.float32)
        mean = drift[4 * k:4 * k + 4].reshape(64, WIDTH).astype(jnp.float32)
        nxt = outer_momentum * mom4[fr, rows, :] + mean
        momn[rows, :] = nxt
        glob = anc + outer_rate * (outer_momentum * nxt + mean)
        local = cur[4 * k:4 * k + 4].reshape(64, WIDTH).astype(jnp.float32)
        new = (blend_local * local + (1.0 - blend_local) * glob).astype(jnp.bfloat16)
        w[fsdp, 4 * k:4 * k + 4] = new.reshape(4, G, WIDTH)

    def send_own(p):
        to_z(y, z, p, has_up, has_dn)
        to_y(y, z, p)

    exchange(0)
    exchange(1)
    loads[2].wait()
    own(0)
    send_own(0)
    exchange(2)
    own(1)
    send_own(1)
    sib(y, z, 0).start()
    exchange(3)
    own(2)
    own(3)
    send_own(2)
    to_y(y, z, YP)
    sib(y, z, 1).start()
    for out in outs:
        out.start()

    low = z < 2
    zm = jnp.where(low, z, 3 - z)

    def zo(j):
        if j == 0:
            return z
        m = j if j > 1 else jnp.where(zm == 0, 1, 0)
        return jnp.where(low, m, 3 - m)

    oz = [zo(j) for j in range(4)]
    go_up = [None] + [(oz[j] < z) & has_up for j in (1, 2, 3)]
    go_dn = [None] + [(oz[j] > z) & has_dn for j in (1, 2, 3)]

    def zz(j, p):
        arrive(y, oz[j], p, 0, PIECES[p])
        to_z(y, oz[j], p, go_up[j], go_dn[j])
        to_y(y, oz[j], p)

    def zy(j, p):
        arrive(y_dn, oz[j], p, 0, PIECES[p])
        go(0, dev_yu, y_dn, oz[j], p, 0, PARTS[p][0]).start()
        arrive(y_up, oz[j], p, 0, PIECES[p])
        go(1, dev_yd, y_up, oz[j], p, 1, PARTS[p][1]).start()

    def zy_far(j, p):
        arrive(y_far, oz[j], p, 0, PARTS[p][0])
        arrive(y_far, oz[j], p, 1, PARTS[p][1])

    def yz(j):
        for oy in (y, y_up, y_dn, y_far):
            arrive(oy, oz[j], YP, 0, PIECES[YP])
            to_z(oy, oz[j], YP, go_up[j], go_dn[j])

    def sib_group(j, half):
        for oy in (y, y_up, y_dn, y_far):
            if j == 0 and oy is y:
                continue
            sib(oy, oz[j], half).start()

    def multiply(j, half):
        def unit(oy, _):
            sib_wait(oy, oz[j], half)
            f = oy * 8 + oz[j] * 2
            a0 = tok[:, pl.ds(pl.multiple_of(f * ROWS + half * 128, 128), 128)]
            a1 = tok[:, pl.ds(pl.multiple_of((f + 1) * ROWS + half * 128, 128), 128)]
            b0 = w[f, 8 * half:8 * half + 8].reshape(128, WIDTH)
            b1 = w[f + 1, 8 * half:8 * half + 8].reshape(128, WIDTH)
            acc[...] += jnp.dot(
                jnp.concatenate([a0, a1], axis=1), jnp.concatenate([b0, b1], axis=0),
                preferred_element_type=jnp.float32,
            )
            return 0

        lax.fori_loop(0, 4, unit, 0)

    for p in range(3):
        zz(1, p)
        zy(0, p)
    zy(0, YP)
    for p in range(3):
        zz(2, p)
    for p in range(3):
        zz(3, p)
        zy(1, p)
    to_z(y, z, YP, has_up, has_dn)
    to_z(y_up, z, YP, has_up, has_dn)
    to_z(y_dn, z, YP, has_up, has_dn)
    for p in range(4):
        zy_far(0, p)
    to_z(y_far, z, YP, has_up, has_dn)
    sib_group(0, 0)
    sib_group(0, 1)
    loads[3].wait()
    multiply(0, 0)
    yz(1)
    multiply(0, 1)
    for p in range(3):
        zy(2, p)
    zy_far(1, 0)
    zy_far(1, 1)
    zy_far(1, 2)
    sib_group(1, 0)
    sib_group(1, 1)
    multiply(1, 0)
    yz(2)
    multiply(1, 1)
    for p in range(3):
        zy(3, p)
    for p in range(3):
        zy_far(2, p)
    sib_group(2, 0)
    sib_group(2, 1)
    multiply(2, 0)
    multiply(2, 1)
    zy_far(3, 0)
    zy_far(3, 1)
    sib_group(3, 0)
    multiply(3, 0)
    yz(3)
    zy_far(3, 2)
    sib_group(3, 1)
    multiply(3, 1)
    keys[...] = (acc[...] * (1.0 / math.sqrt(D))).astype(jnp.bfloat16)

    for k in range(CHUNKS):
        s_copy(k).wait_send()
        for d in range(3):
            raw_copy(k, d).wait_send()
            d_copy(k, d).wait_send()

    flat = w.reshape(32 * 16 * G, WIDTH)

    def sent(sem, rows):
        ref = flat.at[pl.ds(0, rows)]
        remote(ref, ref, sem, g_rs.at[0, 0, 0], dev_sib).wait_send()

    sent(g_ss.at[0], 4 * (ZROWS + PLUS[0]) + YROWS + PLUS[1])
    sent(g_ss.at[1], 4 * (ZROWS + MINUS[0]) + YROWS + MINUS[1])
    for at_z in range(3):
        @pl.when(z == at_z)
        def _(at_z=at_z):
            sent(g_ss.at[2], (at_z + 1) * (ZROWS + 4 * YROWS))

        @pl.when(z == 3 - at_z)
        def _(at_z=at_z):
            sent(g_ss.at[3], (at_z + 1) * (ZROWS + 4 * YROWS))
    sent(sib_ss.at[0], 16 * ROWS)
    for out in outs:
        out.wait()


def fused(current, anchor, momentum, tokens, fragment):
    bf, f32 = jnp.bfloat16, jnp.float32
    dma = pltpu.SemaphoreType.DMA
    return pl.pallas_call(
        kernel,
        out_shape=(
            jax.ShapeDtypeStruct((512, WIDTH), bf),
            jax.ShapeDtypeStruct((16, G, WIDTH), bf),
            jax.ShapeDtypeStruct((ROWS, WIDTH), f32),
        ),
        in_specs=[pl.BlockSpec(memory_space=pltpu.SMEM)] + [pl.BlockSpec(memory_space=pl.ANY)] * 4,
        out_specs=(
            pl.BlockSpec(memory_space=pltpu.VMEM),
            pl.BlockSpec(memory_space=pl.ANY),
            pl.BlockSpec(memory_space=pl.ANY),
        ),
        scratch_shapes=[
            pltpu.VMEM((4, ROWS, WIDTH), bf),
            pltpu.VMEM((4, ROWS, WIDTH), bf),
            pltpu.VMEM((4, ROWS, WIDTH), f32),
            pltpu.VMEM((512, D), bf),
            pltpu.VMEM((32, 16, G, WIDTH), bf),
            pltpu.VMEM((16, G, WIDTH), bf),
            pltpu.VMEM((3, CHUNKS, G, WIDTH), bf),
            pltpu.VMEM((CHUNKS, G, WIDTH), bf),
            pltpu.VMEM((CHUNKS, G, WIDTH), bf),
            pltpu.VMEM((16, G, WIDTH), bf),
            pltpu.VMEM((ROWS, WIDTH), f32),
            pltpu.VMEM((512, WIDTH), f32),
            dma((4,)), dma((2,)),
            dma((3, CHUNKS)), dma((3, CHUNKS)), dma((CHUNKS,)), dma((CHUNKS,)),
            dma((3, CHUNKS)), dma((3, CHUNKS)),
            dma((4,)), dma((16, 4, 2)), dma((1,)), dma((16, 2)),
        ],
        compiler_params=pltpu.CompilerParams(
            collective_id=0, has_side_effects=True, vmem_limit_bytes=48 * 2**20
        ),
    )(fragment, current, anchor, momentum, tokens)


def place_kernel(frag, cur, mom, keys_in, blended, momn, new_cur, new_mom, keys, sem):
    fr = frag[0]
    copy = pltpu.make_async_copy(keys_in, keys, sem.at[8])
    copy.start()
    for i in range(4):
        @pl.when(fr == i)
        def _(i=i):
            pltpu.make_async_copy(momn, new_mom.at[i], sem.at[i]).start()
            pltpu.make_async_copy(blended, new_cur.at[0, i], sem.at[4 + i]).start()

        @pl.when(fr != i)
        def _(i=i):
            pltpu.make_async_copy(mom.at[i], new_mom.at[i], sem.at[i]).start()
            pltpu.make_async_copy(cur.at[0, i], new_cur.at[0, i], sem.at[4 + i]).start()
    for i in range(4):
        pltpu.make_async_copy(mom.at[i], new_mom.at[i], sem.at[i]).wait()
        pltpu.make_async_copy(cur.at[0, i], new_cur.at[0, i], sem.at[4 + i]).wait()
    copy.wait()


def local(current, anchor, momentum, tokens, fragment):
    keys, blended, mom_next = fused(current, anchor, momentum, tokens, fragment)
    return pl.pallas_call(
        place_kernel,
        out_shape=(
            jax.ShapeDtypeStruct(current.shape, current.dtype),
            jax.ShapeDtypeStruct(momentum.shape, momentum.dtype),
            jax.ShapeDtypeStruct(keys.shape, keys.dtype),
        ),
        in_specs=[pl.BlockSpec(memory_space=pltpu.SMEM)] + [pl.BlockSpec(memory_space=pl.ANY)] * 5,
        out_specs=tuple([pl.BlockSpec(memory_space=pl.ANY)] * 3),
        scratch_shapes=[pltpu.SemaphoreType.DMA((9,))],
    )(fragment, current, momentum, keys, blended.reshape(ROWS, WIDTH), mom_next)


def solution(mesh):
    placed = (
        P("island", None, "fsdp", None),
        P(None, "fsdp", None),
        P(None, "fsdp", None),
        P(("island", "fsdp"), None),
        P(),
    )
    return jax.shard_map(
        local,
        mesh=mesh,
        in_specs=placed,
        out_specs=(
            P("island", None, "fsdp", None),
            P(None, "fsdp", None),
            P(("island", "fsdp"), None),
        ),
        check_vma=False,
    )
```

```python
import math

import jax
import jax.numpy as jnp
from jax import lax
from jax.experimental import pallas as pl
from jax.experimental.pallas import tpu as pltpu
from jax.sharding import PartitionSpec as P

D = 8192
WIDTH = 512
ROWS = 256
G = 16
CHUNKS = 4
MESH = pl.DeviceIdType.MESH
VMEM = 60 * 2**20

outer_momentum = 0.9
outer_rate = 0.7
blend_local = 0.5

PIECES = ((0, 4), (4, 4), (8, 5), (13, 3))
PARTS = (((0, 2), (2, 2)), ((4, 2), (6, 2)), ((8, 3), (11, 2)), ((13, 1), (14, 2)))
YP = 3
ZROWS = 13 * G
YROWS = 3 * G
PLUS = [sum(PARTS[p][0][1] for p in range(3)) * G, PARTS[YP][0][1] * G]
MINUS = [sum(PARTS[p][1][1] for p in range(3)) * G, PARTS[YP][1][1] * G]


def kernel(frag, cur_hbm, anc_hbm, mom_hbm, tok_hbm,
           keys, cur_out, mom_out,
           cur4, anc4, mom4, tok, w, cur, raw, s_out, s_in, drift, keys_v, acc,
           load_sem, out_sem, raw_ss, raw_rs, s_ss, s_rs, d_ss, d_rs,
           g_ss, g_rs, sib_ss, sib_rs):
    island = lax.axis_index("island")
    fsdp = lax.axis_index("fsdp")
    zh, x = island // 4, island % 4
    y, z, c = fsdp // 8, (fsdp // 2) % 4, fsdp % 2

    def at(zh_, x_, y_, z_, c_):
        return (zh_ * 4 + x_, y_ * 8 + z_ * 2 + c_)

    y_up, y_dn, y_far = (y + 1) % 4, (y + 3) % 4, (y + 2) % 4
    has_up, has_dn = z < 3, z > 0
    z_up, z_dn = jnp.minimum(z + 1, 3), jnp.maximum(z - 1, 0)
    dev_yu, dev_yd = at(zh, x, y_up, z, c), at(zh, x, y_dn, z, c)
    dev_zu, dev_zd = at(zh, x, y, z_up, c), at(zh, x, y, z_dn, c)
    dev_sib = at(zh, x, y, z, 1 - c)
    dev_far = at(1 - zh, x, y, z, c)
    dev_x = [at(zh, (x + d) % 4, y, z, c) for d in (1, 2, 3)]

    loads = [
        pltpu.make_async_copy(cur_hbm.at[0], cur4, load_sem.at[0]),
        pltpu.make_async_copy(anc_hbm, anc4, load_sem.at[1]),
        pltpu.make_async_copy(mom_hbm, mom4, load_sem.at[2]),
        pltpu.make_async_copy(tok_hbm, tok, load_sem.at[3]),
    ]
    for load in loads:
        load.start()

    barrier = pltpu.get_barrier_semaphore()
    for dev in (*dev_x, dev_far, dev_yu, dev_yd, dev_sib):
        pl.semaphore_signal(barrier, inc=1, device_id=dev, device_id_type=MESH)

    @pl.when(has_up)
    def _():
        pl.semaphore_signal(barrier, inc=1, device_id=dev_zu, device_id_type=MESH)

    @pl.when(has_dn)
    def _():
        pl.semaphore_signal(barrier, inc=1, device_id=dev_zd, device_id_type=MESH)

    ends = jnp.where(has_up, 1, 0) + jnp.where(has_dn, 1, 0)

    fr = frag[0]
    loads[0].wait()
    cur[...] = cur4[fr].reshape(16, G, WIDTH)
    pl.semaphore_wait(barrier, 7 + ends)

    def remote(src, dst, ss, rs, dev):
        return pltpu.make_async_remote_copy(
            src_ref=src, dst_ref=dst, send_sem=ss, recv_sem=rs,
            device_id=dev, device_id_type=MESH,
        )

    def raw_copy(k, d):
        to = (x + d + 1) % 4
        return remote(cur.at[4 * k + to], raw.at[d, k], raw_ss.at[d, k], raw_rs.at[d, k], dev_x[d])

    def s_copy(k):
        return remote(s_out.at[k], s_in.at[k], s_ss.at[k], s_rs.at[k], dev_far)

    def d_copy(k, d):
        mine = 4 * k + x
        return remote(drift.at[mine], drift.at[mine], d_ss.at[d, k], d_rs.at[d, k], dev_x[d])

    def d_wait(k, d):
        theirs = 4 * k + (x + 3 - d) % 4
        remote(drift.at[theirs], drift.at[theirs], d_ss.at[d, k], d_rs.at[d, k], dev_x[d]).wait_recv()

    for k in range(CHUNKS):
        for d in range(3):
            raw_copy(k, d).start()
    acc[...] = jnp.zeros_like(acc)
    loads[1].wait()
    for k in range(CHUNKS):
        for d in range(3):
            raw_copy(k, d).wait_recv()
        mine = 4 * k + x
        anc = anc4[fr, pl.ds(pl.multiple_of(mine * G, G), G), :].astype(jnp.float32)
        total = cur[mine].astype(jnp.float32) - anc
        for d in range(3):
            total += raw[d, k].astype(jnp.float32) - anc
        s_out[k] = total.astype(jnp.bfloat16)
        s_copy(k).start()

    def exchange(k):
        s_copy(k).wait_recv()
        both = s_out[k].astype(jnp.float32) + s_in[k].astype(jnp.float32)
        drift[4 * k + x] = both * 0.125
        for d in range(3):
            d_copy(k, d).start()

    def block(oy, oz, first, count):
        return w.at[oy * 8 + oz * 2 + c, pl.ds(first, count)]

    def go(t, dev, oy, oz, p, h, span):
        ref = block(oy, oz, *span)
        return remote(ref, ref, g_ss.at[t], g_rs.at[oy * 4 + oz, p, h], dev)

    def arrive(oy, oz, p, h, span):
        go(0, dev_yu, oy, oz, p, h, span).wait_recv()

    def to_y(oy, oz, p):
        go(0, dev_yu, oy, oz, p, 0, PIECES[p]).start()
        go(1, dev_yd, oy, oz, p, 0, PIECES[p]).start()

    def to_z(oy, oz, p, up, dn):
        if up is not None:
            @pl.when(up)
            def _():
                go(2, dev_zu, oy, oz, p, 0, PIECES[p]).start()
        if dn is not None:
            @pl.when(dn)
            def _():
                go(3, dev_zd, oy, oz, p, 0, PIECES[p]).start()

    def sib(oy, oz, half):
        ref = block(oy, oz, 8 * half, 8)
        return remote(ref, ref, sib_ss.at[0], sib_rs.at[oy * 4 + oz, half], dev_sib)

    def sib_wait(oy, oz, half):
        ref = w.at[oy * 8 + oz * 2 + 1 - c, pl.ds(8 * half, 8)]
        remote(ref, ref, sib_ss.at[0], sib_rs.at[oy * 4 + oz, half], dev_sib).wait_recv()

    outs = [
        pltpu.make_async_copy(cur4, cur_out.at[0], out_sem.at[0]),
        pltpu.make_async_copy(mom4, mom_out, out_sem.at[1]),
    ]

    def own(k):
        for d in range(3):
            d_wait(k, d)
        rows = pl.ds(64 * k, 64)
        anc = anc4[fr, rows, :].astype(jnp.float32)
        mean = drift[4 * k:4 * k + 4].reshape(64, WIDTH)
        nxt = outer_momentum * mom4[fr, rows, :] + mean
        glob = anc + outer_rate * (outer_momentum * nxt + mean)
        local = cur[4 * k:4 * k + 4].reshape(64, WIDTH).astype(jnp.float32)
        new = (blend_local * local + (1.0 - blend_local) * glob).astype(jnp.bfloat16)
        w[fsdp, 4 * k:4 * k + 4] = new.reshape(4, G, WIDTH)
        return nxt

    def place(k, nxt):
        rows = pl.ds(64 * k, 64)
        new = w[fsdp, 4 * k:4 * k + 4].reshape(64, WIDTH)
        for i in range(4):
            mom4[i, rows, :] = jnp.where(fr == i, nxt, mom4[i, rows, :])
            cur4[i, rows, :] = jnp.where(fr == i, new, cur4[i, rows, :])

    def send_own(p):
        to_z(y, z, p, has_up, has_dn)
        to_y(y, z, p)

    exchange(0)
    exchange(1)
    loads[2].wait()
    nxt0 = own(0)
    send_own(0)
    exchange(2)
    nxt1 = own(1)
    send_own(1)
    sib(y, z, 0).start()
    exchange(3)
    nxt2 = own(2)
    nxt3 = own(3)
    send_own(2)
    to_y(y, z, YP)
    sib(y, z, 1).start()
    for k, nxt in enumerate((nxt0, nxt1, nxt2, nxt3)):
        place(k, nxt)
    for out in outs:
        out.start()

    low = z < 2
    zm = jnp.where(low, z, 3 - z)

    def zo(j):
        if j == 0:
            return z
        m = j if j > 1 else jnp.where(zm == 0, 1, 0)
        return jnp.where(low, m, 3 - m)

    oz = [zo(j) for j in range(4)]
    go_up = [None] + [(oz[j] < z) & has_up for j in (1, 2, 3)]
    go_dn = [None] + [(oz[j] > z) & has_dn for j in (1, 2, 3)]

    def zz(j, p):
        arrive(y, oz[j], p, 0, PIECES[p])
        to_z(y, oz[j], p, go_up[j], go_dn[j])
        to_y(y, oz[j], p)

    def zy(j, p):
        arrive(y_dn, oz[j], p, 0, PIECES[p])
        go(0, dev_yu, y_dn, oz[j], p, 0, PARTS[p][0]).start()
        arrive(y_up, oz[j], p, 0, PIECES[p])
        go(1, dev_yd, y_up, oz[j], p, 1, PARTS[p][1]).start()

    def zy_far(j, p):
        arrive(y_far, oz[j], p, 0, PARTS[p][0])
        arrive(y_far, oz[j], p, 1, PARTS[p][1])

    def yz(j):
        for oy in (y, y_up, y_dn, y_far):
            arrive(oy, oz[j], YP, 0, PIECES[YP])
            to_z(oy, oz[j], YP, go_up[j], go_dn[j])

    def sib_group(j, half):
        for oy in (y, y_up, y_dn, y_far):
            if j == 0 and oy is y:
                continue
            sib(oy, oz[j], half).start()

    def multiply(j, half):
        def unit(oy, _):
            sib_wait(oy, oz[j], half)
            f = oy * 8 + oz[j] * 2
            a0 = tok[:, pl.ds(pl.multiple_of(f * ROWS + half * 128, 128), 128)]
            a1 = tok[:, pl.ds(pl.multiple_of((f + 1) * ROWS + half * 128, 128), 128)]
            b0 = w[f, 8 * half:8 * half + 8].reshape(128, WIDTH)
            b1 = w[f + 1, 8 * half:8 * half + 8].reshape(128, WIDTH)
            acc[...] += jnp.dot(
                jnp.concatenate([a0, a1], axis=1), jnp.concatenate([b0, b1], axis=0),
                preferred_element_type=jnp.float32,
            )
            return 0

        lax.fori_loop(0, 4, unit, 0)

    for p in range(3):
        zz(1, p)
        zy(0, p)
    zy(0, YP)
    for p in range(3):
        zz(2, p)
    for p in range(3):
        zz(3, p)
        zy(1, p)
    to_z(y, z, YP, has_up, has_dn)
    to_z(y_up, z, YP, has_up, has_dn)
    to_z(y_dn, z, YP, has_up, has_dn)
    for p in range(4):
        zy_far(0, p)
    to_z(y_far, z, YP, has_up, has_dn)
    sib_group(0, 0)
    sib_group(0, 1)
    loads[3].wait()
    multiply(0, 0)
    yz(1)
    multiply(0, 1)
    for p in range(3):
        zy(2, p)
    zy_far(1, 0)
    zy_far(1, 1)
    zy_far(1, 2)
    sib_group(1, 0)
    sib_group(1, 1)
    multiply(1, 0)
    yz(2)
    multiply(1, 1)
    for p in range(3):
        zy(3, p)
    for p in range(3):
        zy_far(2, p)
    sib_group(2, 0)
    sib_group(2, 1)
    multiply(2, 0)
    multiply(2, 1)
    zy_far(3, 0)
    zy_far(3, 1)
    sib_group(3, 0)
    multiply(3, 0)
    yz(3)
    zy_far(3, 2)
    sib_group(3, 1)
    multiply(3, 1)
    keys_v[...] = (acc[...] * (1.0 / math.sqrt(D))).astype(jnp.bfloat16)
    last = pltpu.make_async_copy(keys_v, keys, out_sem.at[2])
    last.start()

    for k in range(CHUNKS):
        s_copy(k).wait_send()
        for d in range(3):
            raw_copy(k, d).wait_send()
            d_copy(k, d).wait_send()

    flat = w.reshape(32 * 16 * G, WIDTH)

    def sent(sem, rows):
        ref = flat.at[pl.ds(0, rows)]
        remote(ref, ref, sem, g_rs.at[0, 0, 0], dev_sib).wait_send()

    sent(g_ss.at[0], 4 * (ZROWS + PLUS[0]) + YROWS + PLUS[1])
    sent(g_ss.at[1], 4 * (ZROWS + MINUS[0]) + YROWS + MINUS[1])
    for at_z in range(3):
        @pl.when(z == at_z)
        def _(at_z=at_z):
            sent(g_ss.at[2], (at_z + 1) * (ZROWS + 4 * YROWS))

        @pl.when(z == 3 - at_z)
        def _(at_z=at_z):
            sent(g_ss.at[3], (at_z + 1) * (ZROWS + 4 * YROWS))
    sent(sib_ss.at[0], 16 * ROWS)
    for out in outs:
        out.wait()
    last.wait()


def fused(current, anchor, momentum, tokens, fragment):
    bf, f32 = jnp.bfloat16, jnp.float32
    dma = pltpu.SemaphoreType.DMA
    return pl.pallas_call(
        kernel,
        out_shape=(
            jax.ShapeDtypeStruct((512, WIDTH), bf),
            jax.ShapeDtypeStruct((1, 4, ROWS, WIDTH), bf),
            jax.ShapeDtypeStruct((4, ROWS, WIDTH), f32),
        ),
        in_specs=[pl.BlockSpec(memory_space=pltpu.SMEM)] + [pl.BlockSpec(memory_space=pltpu.HBM)] * 4,
        out_specs=tuple([pl.BlockSpec(memory_space=pl.ANY)] * 3),
        scratch_shapes=[
            pltpu.VMEM((4, ROWS, WIDTH), bf),
            pltpu.VMEM((4, ROWS, WIDTH), bf),
            pltpu.VMEM((4, ROWS, WIDTH), f32),
            pltpu.VMEM((512, D), bf),
            pltpu.VMEM((32, 16, G, WIDTH), bf),
            pltpu.VMEM((16, G, WIDTH), bf),
            pltpu.VMEM((3, CHUNKS, G, WIDTH), bf),
            pltpu.VMEM((CHUNKS, G, WIDTH), bf),
            pltpu.VMEM((CHUNKS, G, WIDTH), bf),
            pltpu.VMEM((16, G, WIDTH), f32),
            pltpu.VMEM((512, WIDTH), bf),
            pltpu.VMEM((512, WIDTH), f32),
            dma((4,)), dma((3,)),
            dma((3, CHUNKS)), dma((3, CHUNKS)), dma((CHUNKS,)), dma((CHUNKS,)),
            dma((3, CHUNKS)), dma((3, CHUNKS)),
            dma((4,)), dma((16, 4, 2)), dma((1,)), dma((16, 2)),
        ],
        compiler_params=pltpu.CompilerParams(
            collective_id=0, has_side_effects=True, vmem_limit_bytes=VMEM
        ),
    )(fragment, current, anchor, momentum, tokens)


def place_kernel(cur_in, mom_in, keys_in, cur, mom, keys):
    cur[...] = cur_in[...]
    mom[...] = mom_in[...]
    keys[...] = keys_in[...]


def local(current, anchor, momentum, tokens, fragment):
    keys, new_current, new_momentum = fused(current, anchor, momentum, tokens, fragment)
    shapes = [jax.ShapeDtypeStruct(a.shape, a.dtype) for a in (new_current, new_momentum, keys)]
    specs = [
        pl.BlockSpec((1, 4, ROWS // 2, WIDTH), lambda i: (0, 0, i, 0)),
        pl.BlockSpec((4, ROWS // 2, WIDTH), lambda i: (0, i, 0)),
        pl.BlockSpec((ROWS, WIDTH), lambda i: (i, 0)),
    ]
    return pl.pallas_call(
        place_kernel,
        out_shape=tuple(shapes),
        grid=(2,),
        in_specs=specs,
        out_specs=tuple(specs),
        compiler_params=pltpu.CompilerParams(vmem_limit_bytes=VMEM),
    )(new_current, new_momentum, keys)


def solution(mesh):
    placed = (
        P("island", None, "fsdp", None),
        P(None, "fsdp", None),
        P(None, "fsdp", None),
        P(("island", "fsdp"), None),
        P(),
    )
    return jax.shard_map(
        local,
        mesh=mesh,
        in_specs=placed,
        out_specs=(
            P("island", None, "fsdp", None),
            P(None, "fsdp", None),
            P(("island", "fsdp"), None),
        ),
        check_vma=False,
    )
```

```python
import math

import jax
import jax.numpy as jnp
from jax import lax
from jax.experimental import pallas as pl
from jax.experimental.pallas import tpu as pltpu
from jax.sharding import PartitionSpec as P

D = 8192
WIDTH = 512
ROWS = 256
G = 16
CHUNKS = 4
MESH = pl.DeviceIdType.MESH
VMEM = 60 * 2**20

outer_momentum = 0.9
outer_rate = 0.7
blend_local = 0.5

HALF = 8
A_PIECES, A_PARTS = ((0, 5), (5, 3)), (((0, 3), (3, 2)), ((5, 1), (6, 2)))
B_PIECES, B_PARTS = ((0, 4), (4, 4)), (((0, 2), (2, 2)), ((4, 2), (6, 2)))
ZP, YP = 0, 1


def kernel(frag, cur_hbm, anc_hbm, mom_hbm, tok_hbm,
           keys, cur_out, mom_out,
           cur4, anc4, mom4, tok, ra, wa, wb, gb, cur, raw, s_out, s_in, drift, keys_v, acc,
           load_sem, out_sem, raw_ss, raw_rs, s_ss, s_rs, d_ss, d_rs,
           send_sem, a_rs, b_rs, g_rs, x_rs, sib_rs):
    island = lax.axis_index("island")
    fsdp = lax.axis_index("fsdp")
    zh, x = island // 4, island % 4
    y, z, c = fsdp // 8, (fsdp // 2) % 4, fsdp % 2

    def at(zh_, x_, y_, z_, c_):
        return (zh_ * 4 + x_, y_ * 8 + z_ * 2 + c_)

    low = z < 2
    zm = jnp.where(low, z, 3 - z)

    def zo(j):
        if j == 0:
            return z
        m = j if j > 1 else jnp.where(zm == 0, 1, 0)
        return jnp.where(low, m, 3 - m)

    oz = [zo(j) for j in range(4)]
    y_up, y_dn, y_far = (y + 1) % 4, (y + 3) % 4, (y + 2) % 4
    has_up, has_dn = z < 3, z > 0
    z_up, z_dn = jnp.minimum(z + 1, 3), jnp.maximum(z - 1, 0)
    dev_yu, dev_yd, dev_yf = (at(zh, x, o, z, c) for o in (y_up, y_dn, y_far))
    dev_zu, dev_zd = at(zh, x, y, z_up, c), at(zh, x, y, z_dn, c)
    dev_z = [None] + [at(zh, x, y, oz[j], c) for j in (1, 2, 3)]
    dev_sib = at(zh, x, y, z, 1 - c)
    dev_far = at(1 - zh, x, y, z, c)
    dev_x = [at(zh, (x + d) % 4, y, z, c) for d in (1, 2, 3)]

    loads = [
        pltpu.make_async_copy(cur_hbm.at[0], cur4, load_sem.at[0]),
        pltpu.make_async_copy(anc_hbm, anc4, load_sem.at[1]),
        pltpu.make_async_copy(mom_hbm, mom4, load_sem.at[2]),
        pltpu.make_async_copy(tok_hbm, tok, load_sem.at[3]),
    ]
    for load in loads:
        load.start()

    barrier = pltpu.get_barrier_semaphore()
    peers = (*dev_x, dev_far, dev_yu, dev_yd, dev_yf, *dev_z[1:], dev_sib)
    for dev in peers:
        pl.semaphore_signal(barrier, inc=1, device_id=dev, device_id_type=MESH)

    fr = frag[0]
    loads[0].wait()
    whole = cur4[fr].reshape(16, G, WIDTH)
    cur[...] = whole
    ra[z, y] = whole[:HALF]
    pl.semaphore_wait(barrier, len(peers))

    def remote(src, dst, ss, rs, dev):
        return pltpu.make_async_remote_copy(
            src_ref=src, dst_ref=dst, send_sem=ss, recv_sem=rs,
            device_id=dev, device_id_type=MESH,
        )

    def raw_copy(k, d):
        to = (x + d + 1) % 4
        return remote(cur.at[4 * k + to], raw.at[d, k], raw_ss.at[d, k], raw_rs.at[d, k], dev_x[d])

    def send_raw(k):
        for d in range(3):
            raw_copy(k, d).start()

    def s_copy(k):
        return remote(s_out.at[k], s_in.at[k], s_ss.at[k], s_rs.at[k], dev_far)

    def d_copy(k, d):
        mine = 4 * k + x
        return remote(drift.at[mine], drift.at[mine], d_ss.at[d, k], d_rs.at[d, k], dev_x[d])

    def d_wait(k, d):
        theirs = 4 * k + (x + 3 - d) % 4
        remote(drift.at[theirs], drift.at[theirs], d_ss.at[d, k], d_rs.at[d, k], dev_x[d]).wait_recv()

    def island_sum(k):
        for d in range(3):
            raw_copy(k, d).wait_recv()
        mine = 4 * k + x
        anc = anc4[fr, pl.ds(pl.multiple_of(mine * G, G), G), :].astype(jnp.float32)
        total = cur[mine].astype(jnp.float32) - anc
        for d in range(3):
            total += raw[d, k].astype(jnp.float32) - anc
        s_out[k] = total.astype(jnp.bfloat16)
        s_copy(k).start()

    def step(anc, mom, mean):
        nxt = outer_momentum * mom + mean
        return nxt, anc + outer_rate * (outer_momentum * nxt + mean)

    def exchange(k):
        s_copy(k).wait_recv()
        both = s_out[k].astype(jnp.float32) + s_in[k].astype(jnp.float32)
        drift[4 * k + x] = both * 0.125

    def share(k):
        for d in range(3):
            d_copy(k, d).start()

    def own_global(k):
        rows = pl.ds(pl.multiple_of((4 * k + x) * G, G), G)
        _, glob = step(anc4[fr, rows, :].astype(jnp.float32), mom4[fr, rows, :], drift[4 * k + x])
        gb[z, x, y, k] = glob.astype(jnp.bfloat16)

    def own(k):
        for d in range(3):
            d_wait(k, d)
        rows = pl.ds(64 * k, 64)
        mean = drift[4 * k:4 * k + 4].reshape(64, WIDTH)
        nxt, glob = step(anc4[fr, rows, :].astype(jnp.float32), mom4[fr, rows, :], mean)
        local = cur[4 * k:4 * k + 4].reshape(64, WIDTH).astype(jnp.float32)
        new = (blend_local * local + (1.0 - blend_local) * glob).astype(jnp.bfloat16)
        if k >= 2:
            wb[z, c, y, 4 * k - 8:4 * k - 4] = new.reshape(4, G, WIDTH)
        return nxt, new

    def place(k, nxt, new):
        rows = pl.ds(64 * k, 64)
        for i in range(4):
            mom4[i, rows, :] = jnp.where(fr == i, nxt, mom4[i, rows, :])
            cur4[i, rows, :] = jnp.where(fr == i, new, cur4[i, rows, :])

    outs = [
        pltpu.make_async_copy(cur4, cur_out.at[0], out_sem.at[0]),
        pltpu.make_async_copy(mom4, mom_out, out_sem.at[1]),
    ]

    def block(kind, oy, ozj, span):
        if kind == 0:
            return ra.at[ozj, oy, pl.ds(*span)]
        return wb.at[ozj, c, oy, pl.ds(*span)]

    pieces, parts, arrived = (A_PIECES, B_PIECES), (A_PARTS, B_PARTS), (a_rs, b_rs)

    def go(t, dev, kind, oy, ozj, p, h, span):
        ref = block(kind, oy, ozj, span)
        return remote(ref, ref, send_sem.at[t], arrived[kind].at[ozj * 4 + oy, p, h], dev)

    def arrive(kind, oy, ozj, p, h, span):
        go(0, dev_yu, kind, oy, ozj, p, h, span).wait_recv()

    def to_y(kind, ozj, p):
        go(0, dev_yu, kind, y, ozj, p, 0, pieces[kind][p]).start()
        go(1, dev_yd, kind, y, ozj, p, 0, pieces[kind][p]).start()

    def to_z(kind, p, j):
        go(2, dev_z[j], kind, y, z, p, 0, pieces[kind][p]).start()

    def zz(kind, j, p):
        arrive(kind, y, oz[j], p, 0, pieces[kind][p])
        to_y(kind, oz[j], p)

    def zyd(kind, j, p):
        arrive(kind, y_dn, oz[j], p, 0, pieces[kind][p])
        go(0, dev_yu, kind, y_dn, oz[j], p, 0, parts[kind][p][0]).start()

    def zyu(kind, j, p):
        arrive(kind, y_up, oz[j], p, 0, pieces[kind][p])
        go(1, dev_yd, kind, y_up, oz[j], p, 1, parts[kind][p][1]).start()

    def zy_far(kind, j, p):
        for h in range(2):
            arrive(kind, y_far, oz[j], p, h, parts[kind][p][h])

    def onward(oy, ozj, up, dn):
        @pl.when(up)
        def _():
            go(3, dev_zu, 0, oy, ozj, YP, 0, A_PIECES[YP]).start()

        @pl.when(dn)
        def _():
            go(4, dev_zd, 0, oy, ozj, YP, 0, A_PIECES[YP]).start()

    def yz(j, oy):
        arrive(0, oy, oz[j], YP, 0, A_PIECES[YP])
        onward(oy, oz[j], (oz[j] < z) & has_up, (oz[j] > z) & has_dn)

    def g_copy(oy, ozj, dev):
        ref = gb.at[ozj, x, oy]
        return remote(ref, ref, send_sem.at[5], g_rs.at[ozj * 4 + oy], dev)

    def g_to_y(ozj):
        for dev in (dev_yu, dev_yd, dev_yf):
            g_copy(y, ozj, dev).start()

    def g_to_z():
        for dev in dev_z[1:]:
            g_copy(y, z, dev).start()

    def zzg(j):
        g_copy(y, oz[j], dev_yu).wait_recv()
        g_to_y(oz[j])

    def x_copy(j, d):
        ref = gb.at[oz[j], x]
        return remote(ref, ref, send_sem.at[6], x_rs.at[oz[j], d], dev_x[d])

    def xg(j):
        for oy in (y_up, y_dn, y_far):
            g_copy(oy, oz[j], dev_yu).wait_recv()
        for d in range(3):
            x_copy(j, d).start()

    def x_wait(j, d):
        ref = gb.at[oz[j], (x + 3 - d) % 4]
        remote(ref, ref, send_sem.at[6], x_rs.at[oz[j], d], dev_x[d]).wait_recv()

    def sib(kind, j):
        ref = (wa, wb)[kind].at[oz[j], c]
        return remote(ref, ref, send_sem.at[7], sib_rs.at[kind, oz[j]], dev_sib)

    def sib_wait(kind, j):
        ref = (wa, wb)[kind].at[oz[j], 1 - c]
        remote(ref, ref, send_sem.at[7], sib_rs.at[kind, oz[j]], dev_sib).wait_recv()

    def blend(j):
        zy_far(0, j, ZP)
        for d in range(3):
            x_wait(j, d)

        def one(oy, _):
            for k in range(2):
                for q in range(4):
                    mix = blend_local * ra[oz[j], oy, 4 * k + q].astype(jnp.float32)
                    mix += (1.0 - blend_local) * gb[oz[j], q, oy, k].astype(jnp.float32)
                    wa[oz[j], c, oy, 4 * k + q] = mix.astype(jnp.bfloat16)
            return 0

        lax.fori_loop(0, 4, one, 0)
        sib(0, j).start()

    def finish(j):
        for p in range(2):
            zy_far(1, j, p)
        sib(1, j).start()

    def multiply(kind, j):
        sib_wait(kind, j)

        cols = [
            pl.ds(pl.multiple_of((oy * 8 + oz[j] * 2 + core) * ROWS + kind * 128, 128), 128)
            for core in range(2) for oy in range(4)
        ]
        rhs = (wa, wb)[kind].at[oz[j]]
        a = jnp.concatenate([tok[:, col] for col in cols], axis=1)
        acc[...] += jnp.dot(a, rhs[...].reshape(1024, WIDTH), preferred_element_type=jnp.float32)

    acc[...] = jnp.zeros_like(acc)
    to_z(0, ZP, 1)
    to_z(0, ZP, 3)
    send_raw(1)
    to_y(0, z, 1)
    to_z(0, ZP, 2)
    send_raw(0)
    send_raw(2)
    loads[1].wait()
    island_sum(2)
    to_y(0, z, 0)
    send_raw(3)
    zyd(0, 0, 1)
    zyu(0, 0, 1)
    island_sum(0)
    island_sum(1)
    zz(0, 2, 0)
    zz(0, 1, 0)
    island_sum(3)
    exchange(2)
    zyd(0, 0, 0)
    exchange(1)
    share(2)
    exchange(0)
    loads[2].wait()
    own_global(1)
    own_global(0)
    g_to_z()
    g_to_y(z)
    zz(0, 3, 0)
    zy_far(0, 0, YP)
    exchange(3)
    onward(y_far, z, has_up, has_dn)
    share(3)
    onward(y, z, has_up, has_dn)
    zyu(0, 2, 0)
    share(1)
    zzg(1)
    own2 = own(2)
    onward(y_dn, z, has_up, has_dn)
    zzg(2)
    to_y(1, z, 0)
    onward(y_up, z, has_up, has_dn)
    to_z(1, 0, 2)
    own3 = own(3)
    to_z(1, 1, 1)
    share(0)
    own1 = own(1)
    zzg(3)
    yz(1, y)
    zyd(0, 1, 0)
    to_z(1, 0, 3)
    zyu(0, 0, 0)
    xg(0)
    zyd(1, 0, 0)
    zyu(0, 1, 0)
    to_y(1, z, 1)
    zz(1, 1, 1)
    xg(1)
    to_z(1, 0, 1)
    to_z(1, 1, 2)
    to_z(1, 1, 3)
    zz(1, 3, 0)
    place(1, *own1)
    xg(2)
    zz(1, 2, 0)
    yz(1, y_up)
    zyd(1, 0, 1)
    zz(1, 1, 0)
    xg(3)
    own0 = own(0)
    place(0, *own0)
    zyu(0, 3, 0)
    zyu(1, 1, 1)
    zz(1, 3, 1)
    yz(2, y_up)
    blend(0)
    zz(1, 2, 1)
    zyd(0, 2, 0)
    zyu(1, 0, 0)
    zyu(1, 3, 0)
    yz(1, y_far)
    zyd(1, 3, 0)
    place(2, *own2)
    yz(2, y_dn)
    yz(1, y_dn)
    zyd(1, 1, 1)
    zyd(1, 1, 0)
    yz(3, y)
    blend(1)
    yz(3, y_up)
    zyu(1, 0, 1)
    zyu(1, 2, 0)
    zyu(1, 1, 0)
    yz(3, y_far)
    zyd(1, 2, 0)
    zyu(1, 2, 1)
    zyd(1, 2, 1)
    zyd(1, 3, 1)
    zyu(1, 3, 1)
    place(3, *own3)
    zyd(0, 3, 0)
    yz(2, y_far)
    loads[3].wait()
    multiply(0, 0)
    yz(3, y_dn)
    multiply(0, 1)
    yz(2, y)
    finish(1)
    finish(2)
    finish(0)
    finish(3)
    blend(2)
    blend(3)
    multiply(1, 0)
    multiply(0, 2)
    multiply(0, 3)
    multiply(1, 1)
    multiply(1, 2)
    for out in outs:
        out.start()
    multiply(1, 3)
    keys_v[...] = (acc[...] * (1.0 / math.sqrt(D))).astype(jnp.bfloat16)
    last = pltpu.make_async_copy(keys_v, keys, out_sem.at[2])
    last.start()

    for k in range(CHUNKS):
        s_copy(k).wait_send()
        for d in range(3):
            raw_copy(k, d).wait_send()
            d_copy(k, d).wait_send()

    flat = wb.reshape(32 * HALF * G, WIDTH)

    def sent(t, groups):
        ref = flat.at[pl.ds(0, groups * G)]
        remote(ref, ref, send_sem.at[t], g_rs.at[0], dev_sib).wait_send()

    def size(kind, p, h=None):
        return pieces[kind][p][1] if h is None else parts[kind][p][h][1]

    zfirst = ((0, ZP), (1, 0), (1, 1))
    for h in range(2):
        sent(h, 4 * sum(size(*kp) + size(*kp, h) for kp in zfirst) + size(0, YP) + size(0, YP, h))
    sent(2, 3 * sum(size(*kp) for kp in zfirst))
    for at_z in range(3):
        @pl.when(z == at_z)
        def _(at_z=at_z):
            sent(3, (at_z + 1) * 4 * size(0, YP))

        @pl.when(z == 3 - at_z)
        def _(at_z=at_z):
            sent(4, (at_z + 1) * 4 * size(0, YP))
    sent(5, 2 * (3 + 3 * 4))
    sent(6, 4 * 3 * 8)
    sent(7, 2 * 4 * 4 * HALF)
    for out in outs:
        out.wait()
    last.wait()


def fused(current, anchor, momentum, tokens, fragment):
    bf, f32 = jnp.bfloat16, jnp.float32
    dma = pltpu.SemaphoreType.DMA
    return pl.pallas_call(
        kernel,
        out_shape=(
            jax.ShapeDtypeStruct((512, WIDTH), bf),
            jax.ShapeDtypeStruct((1, 4, ROWS, WIDTH), bf),
            jax.ShapeDtypeStruct((4, ROWS, WIDTH), f32),
        ),
        in_specs=[pl.BlockSpec(memory_space=pltpu.SMEM)] + [pl.BlockSpec(memory_space=pltpu.HBM)] * 4,
        out_specs=tuple([pl.BlockSpec(memory_space=pl.ANY)] * 3),
        scratch_shapes=[
            pltpu.VMEM((4, ROWS, WIDTH), bf),
            pltpu.VMEM((4, ROWS, WIDTH), bf),
            pltpu.VMEM((4, ROWS, WIDTH), f32),
            pltpu.VMEM((512, D), bf),
            pltpu.VMEM((4, 4, HALF, G, WIDTH), bf),
            pltpu.VMEM((4, 2, 4, HALF, G, WIDTH), bf),
            pltpu.VMEM((4, 2, 4, HALF, G, WIDTH), bf),
            pltpu.VMEM((4, 4, 4, 2, G, WIDTH), bf),
            pltpu.VMEM((16, G, WIDTH), bf),
            pltpu.VMEM((3, CHUNKS, G, WIDTH), bf),
            pltpu.VMEM((CHUNKS, G, WIDTH), bf),
            pltpu.VMEM((CHUNKS, G, WIDTH), bf),
            pltpu.VMEM((16, G, WIDTH), f32),
            pltpu.VMEM((512, WIDTH), bf),
            pltpu.VMEM((512, WIDTH), f32),
            dma((4,)), dma((3,)),
            dma((3, CHUNKS)), dma((3, CHUNKS)), dma((CHUNKS,)), dma((CHUNKS,)),
            dma((3, CHUNKS)), dma((3, CHUNKS)),
            dma((8,)), dma((16, 2, 2)), dma((16, 2, 2)), dma((16,)), dma((4, 3)), dma((2, 4)),
        ],
        compiler_params=pltpu.CompilerParams(
            collective_id=0, has_side_effects=True, vmem_limit_bytes=VMEM
        ),
    )(fragment, current, anchor, momentum, tokens)


def place_kernel(cur_in, mom_in, keys_in, cur, mom, keys):
    cur[...] = cur_in[...]
    mom[...] = mom_in[...]
    keys[...] = keys_in[...]


def local(current, anchor, momentum, tokens, fragment):
    keys, new_current, new_momentum = fused(current, anchor, momentum, tokens, fragment)
    shapes = [jax.ShapeDtypeStruct(a.shape, a.dtype) for a in (new_current, new_momentum, keys)]
    specs = [
        pl.BlockSpec((1, 4, ROWS // 2, WIDTH), lambda i: (0, 0, i, 0)),
        pl.BlockSpec((4, ROWS // 2, WIDTH), lambda i: (0, i, 0)),
        pl.BlockSpec((ROWS, WIDTH), lambda i: (i, 0)),
    ]
    return pl.pallas_call(
        place_kernel,
        out_shape=tuple(shapes),
        grid=(2,),
        in_specs=specs,
        out_specs=tuple(specs),
        compiler_params=pltpu.CompilerParams(vmem_limit_bytes=VMEM),
    )(new_current, new_momentum, keys)


def solution(mesh):
    placed = (
        P("island", None, "fsdp", None),
        P(None, "fsdp", None),
        P(None, "fsdp", None),
        P(("island", "fsdp"), None),
        P(),
    )
    return jax.shard_map(
        local,
        mesh=mesh,
        in_specs=placed,
        out_specs=(
            P("island", None, "fsdp", None),
            P(None, "fsdp", None),
            P(("island", "fsdp"), None),
        ),
        check_vma=False,
    )
```

```python
import math

import jax
import jax.numpy as jnp
from jax import lax
from jax.experimental import pallas as pl
from jax.experimental.pallas import tpu as pltpu
from jax.sharding import PartitionSpec as P

D = 8192
WIDTH = 512
ROWS = 256
G = 16
CHUNKS = 4
MESH = pl.DeviceIdType.MESH
VMEM = 60 * 2**20

outer_momentum = 0.9
outer_rate = 0.7
blend_local = 0.5

HALF = 8
A_PIECES, A_PARTS = ((0, 5), (5, 3)), (((0, 3), (3, 2)), ((5, 1), (6, 2)))
B_PIECES, B_PARTS = ((0, 4), (4, 4)), (((0, 2), (2, 2)), ((4, 2), (6, 2)))
ZP, YP = 0, 1


def kernel(frag, cur_hbm, anc_hbm, mom_hbm, tok_hbm,
           keys, cur_out, mom_out,
           cur4, anc4, mom4, tok, ra, wa, wb, gb, cur, raw, s_out, s_in, drift, keys_v, acc,
           load_sem, out_sem, raw_ss, raw_rs, s_ss, s_rs, d_ss, d_rs,
           send_sem, a_rs, b_rs, g_rs, gh_rs, x_rs, xh_rs, sib_rs, sibb_rs):
    island = lax.axis_index("island")
    fsdp = lax.axis_index("fsdp")
    zh, x = island // 4, island % 4
    y, z, c = fsdp // 8, (fsdp // 2) % 4, fsdp % 2

    def at(zh_, x_, y_, z_, c_):
        return (zh_ * 4 + x_, y_ * 8 + z_ * 2 + c_)

    low = z < 2
    zm = jnp.where(low, z, 3 - z)

    def zo(j):
        if j == 0:
            return z
        m = j if j > 1 else jnp.where(zm == 0, 1, 0)
        return jnp.where(low, m, 3 - m)

    oz = [zo(j) for j in range(4)]
    y_up, y_dn, y_far = (y + 1) % 4, (y + 3) % 4, (y + 2) % 4
    has_up, has_dn = z < 3, z > 0
    z_up, z_dn = jnp.minimum(z + 1, 3), jnp.maximum(z - 1, 0)
    dev_yu, dev_yd = at(zh, x, y_up, z, c), at(zh, x, y_dn, z, c)
    dev_zu, dev_zd = at(zh, x, y, z_up, c), at(zh, x, y, z_dn, c)
    dev_z = [None] + [at(zh, x, y, oz[j], c) for j in (1, 2, 3)]
    dev_sib = at(zh, x, y, z, 1 - c)
    dev_far = at(1 - zh, x, y, z, c)
    dev_x = [at(zh, (x + d) % 4, y, z, c) for d in (1, 2, 3)]

    loads = [
        pltpu.make_async_copy(cur_hbm.at[0], cur4, load_sem.at[0]),
        pltpu.make_async_copy(anc_hbm, anc4, load_sem.at[1]),
        pltpu.make_async_copy(mom_hbm, mom4, load_sem.at[2]),
        pltpu.make_async_copy(tok_hbm, tok, load_sem.at[3]),
    ]
    for load in loads:
        load.start()

    barrier = pltpu.get_barrier_semaphore()
    peers = (*dev_x, dev_far, dev_yu, dev_yd, *dev_z[1:], dev_sib)
    for dev in peers:
        pl.semaphore_signal(barrier, inc=1, device_id=dev, device_id_type=MESH)

    fr = frag[0]
    loads[0].wait()
    whole = cur4[fr].reshape(16, G, WIDTH)
    cur[...] = whole
    ra[z, y] = whole[:HALF]
    pl.semaphore_wait(barrier, len(peers))

    def remote(src, dst, ss, rs, dev):
        return pltpu.make_async_remote_copy(
            src_ref=src, dst_ref=dst, send_sem=ss, recv_sem=rs,
            device_id=dev, device_id_type=MESH,
        )

    def raw_copy(k, d):
        to = (x + d + 1) % 4
        return remote(cur.at[4 * k + to], raw.at[d, k], raw_ss.at[d, k], raw_rs.at[d, k], dev_x[d])

    def send_raw(k):
        for d in range(3):
            raw_copy(k, d).start()

    def s_copy(k):
        return remote(s_out.at[k], s_in.at[k], s_ss.at[k], s_rs.at[k], dev_far)

    def d_copy(k, d):
        mine = 4 * k + x
        return remote(drift.at[mine], drift.at[mine], d_ss.at[d, k], d_rs.at[d, k], dev_x[d])

    def d_wait(k, d):
        theirs = 4 * k + (x + 3 - d) % 4
        remote(drift.at[theirs], drift.at[theirs], d_ss.at[d, k], d_rs.at[d, k], dev_x[d]).wait_recv()

    def island_sum(k):
        for d in range(3):
            raw_copy(k, d).wait_recv()
        mine = 4 * k + x
        anc = anc4[fr, pl.ds(pl.multiple_of(mine * G, G), G), :].astype(jnp.float32)
        total = cur[mine].astype(jnp.float32) - anc
        for d in range(3):
            total += raw[d, k].astype(jnp.float32) - anc
        s_out[k] = total.astype(jnp.bfloat16)
        s_copy(k).start()

    def step(anc, mom, mean):
        nxt = outer_momentum * mom + mean
        return nxt, anc + outer_rate * (outer_momentum * nxt + mean)

    def exchange(k):
        s_copy(k).wait_recv()
        both = s_out[k].astype(jnp.float32) + s_in[k].astype(jnp.float32)
        drift[4 * k + x] = both * 0.125

    def share(k):
        for d in range(3):
            d_copy(k, d).start()

    def own_global(k):
        rows = pl.ds(pl.multiple_of((4 * k + x) * G, G), G)
        _, glob = step(anc4[fr, rows, :].astype(jnp.float32), mom4[fr, rows, :], drift[4 * k + x])
        gb[z, x, y, k] = glob.astype(jnp.bfloat16)

    def own(k):
        for d in range(3):
            d_wait(k, d)
        rows = pl.ds(64 * k, 64)
        mean = drift[4 * k:4 * k + 4].reshape(64, WIDTH)
        nxt, glob = step(anc4[fr, rows, :].astype(jnp.float32), mom4[fr, rows, :], mean)
        local = cur[4 * k:4 * k + 4].reshape(64, WIDTH).astype(jnp.float32)
        new = (blend_local * local + (1.0 - blend_local) * glob).astype(jnp.bfloat16)
        if k >= 2:
            wb[z, c, y, 4 * k - 8:4 * k - 4] = new.reshape(4, G, WIDTH)
        return nxt, new

    def place(k, nxt, new):
        rows = pl.ds(64 * k, 64)
        for i in range(4):
            mom4[i, rows, :] = jnp.where(fr == i, nxt, mom4[i, rows, :])
            cur4[i, rows, :] = jnp.where(fr == i, new, cur4[i, rows, :])

    outs = [
        pltpu.make_async_copy(cur4, cur_out.at[0], out_sem.at[0]),
        pltpu.make_async_copy(mom4, mom_out, out_sem.at[1]),
    ]

    def block(kind, oy, ozj, span):
        if kind == 0:
            return ra.at[ozj, oy, pl.ds(*span)]
        return wb.at[ozj, c, oy, pl.ds(*span)]

    pieces, parts, arrived = (A_PIECES, B_PIECES), (A_PARTS, B_PARTS), (a_rs, b_rs)

    def go(t, dev, kind, oy, ozj, p, h, span):
        ref = block(kind, oy, ozj, span)
        return remote(ref, ref, send_sem.at[t], arrived[kind].at[ozj * 4 + oy, p, h], dev)

    def arrive(kind, oy, ozj, p, h, span):
        go(0, dev_yu, kind, oy, ozj, p, h, span).wait_recv()

    def to_y(kind, ozj, p):
        go(0, dev_yu, kind, y, ozj, p, 0, pieces[kind][p]).start()
        go(1, dev_yd, kind, y, ozj, p, 0, pieces[kind][p]).start()

    def to_z(kind, p, j):
        go(2, dev_z[j], kind, y, z, p, 0, pieces[kind][p]).start()

    def zz(kind, j, p):
        arrive(kind, y, oz[j], p, 0, pieces[kind][p])
        to_y(kind, oz[j], p)

    def zyd(kind, j, p):
        arrive(kind, y_dn, oz[j], p, 0, pieces[kind][p])
        go(0, dev_yu, kind, y_dn, oz[j], p, 0, parts[kind][p][0]).start()

    def zyu(kind, j, p):
        arrive(kind, y_up, oz[j], p, 0, pieces[kind][p])
        go(1, dev_yd, kind, y_up, oz[j], p, 1, parts[kind][p][1]).start()

    def zy_far(kind, j, p):
        for h in range(2):
            arrive(kind, y_far, oz[j], p, h, parts[kind][p][h])

    def onward(oy, ozj, up, dn):
        @pl.when(up)
        def _():
            go(3, dev_zu, 0, oy, ozj, YP, 0, A_PIECES[YP]).start()

        @pl.when(dn)
        def _():
            go(4, dev_zd, 0, oy, ozj, YP, 0, A_PIECES[YP]).start()

    def yz(j, oy):
        arrive(0, oy, oz[j], YP, 0, A_PIECES[YP])
        onward(oy, oz[j], (oz[j] < z) & has_up, (oz[j] > z) & has_dn)

    def g_copy(oy, ozj, dev):
        ref = gb.at[ozj, x, oy]
        return remote(ref, ref, send_sem.at[5], g_rs.at[ozj * 4 + oy], dev)

    def g_part(oy, ozj, k, dev):
        ref = gb.at[ozj, x, oy, k]
        return remote(ref, ref, send_sem.at[5], gh_rs.at[ozj, k], dev)

    def g_to_y(ozj):
        g_copy(y, ozj, dev_yu).start()
        g_copy(y, ozj, dev_yd).start()

    def g_to_z():
        for dev in dev_z[1:]:
            g_copy(y, z, dev).start()

    def zzg(j):
        g_copy(y, oz[j], dev_yu).wait_recv()
        g_to_y(oz[j])

    def gf(j):
        g_copy(y_dn, oz[j], dev_yu).wait_recv()
        g_part(y_dn, oz[j], 0, dev_yu).start()
        g_copy(y_up, oz[j], dev_yu).wait_recv()
        g_part(y_up, oz[j], 1, dev_yd).start()

    def x_copy(j, d, slot, dev):
        ref = gb.at[oz[j], slot]
        return remote(ref, ref, send_sem.at[6], x_rs.at[oz[j], d], dev)

    def x_part(j, d, slot, dev):
        ref = gb.at[oz[j], slot, pl.ds(2 * d, 2)]
        return remote(ref, ref, send_sem.at[6], xh_rs.at[oz[j], d], dev)

    x_up, x_dn, x_far = (x + 1) % 4, (x + 3) % 4, (x + 2) % 4

    def xg(j):
        for k in range(2):
            g_part(y_far, oz[j], k, dev_yu).wait_recv()
        x_copy(j, 0, x, dev_x[0]).start()
        x_copy(j, 1, x, dev_x[2]).start()

    def xf(j):
        x_copy(j, 0, x_dn, dev_x[0]).wait_recv()
        x_part(j, 0, x_dn, dev_x[0]).start()
        x_copy(j, 1, x_up, dev_x[0]).wait_recv()
        x_part(j, 1, x_up, dev_x[2]).start()

    def sib_a(j):
        ref = wa.at[oz[j], c]
        return remote(ref, ref, send_sem.at[7], sib_rs.at[oz[j]], dev_sib)

    def sib_b(j, oy, core):
        ref = wb.at[oz[j], core, oy]
        return remote(ref, ref, send_sem.at[7], sibb_rs.at[oz[j], oy], dev_sib)

    def sib_wait(kind, j):
        if kind == 0:
            ref = wa.at[oz[j], 1 - c]
            remote(ref, ref, send_sem.at[7], sib_rs.at[oz[j]], dev_sib).wait_recv()
        else:
            for oy in range(4):
                sib_b(j, oy, 1 - c).wait_recv()

    def blend(j):
        zy_far(0, j, ZP)
        for d in range(2):
            x_part(j, d, x_far, dev_x[0]).wait_recv()

        def one(oy, _):
            for k in range(2):
                for q in range(4):
                    mix = blend_local * ra[oz[j], oy, 4 * k + q].astype(jnp.float32)
                    mix += (1.0 - blend_local) * gb[oz[j], q, oy, k].astype(jnp.float32)
                    wa[oz[j], c, oy, 4 * k + q] = mix.astype(jnp.bfloat16)
            return 0

        lax.fori_loop(0, 4, one, 0)
        sib_a(j).start()

    def finish(j, r):
        oy = (y, y_up, y_far, y_dn)[r]
        if r == 2:
            for p in range(2):
                zy_far(1, j, p)
        sib_b(j, oy, c).start()

    def multiply(kind, j):
        sib_wait(kind, j)

        cols = [
            pl.ds(pl.multiple_of((oy * 8 + oz[j] * 2 + core) * ROWS + kind * 128, 128), 128)
            for core in range(2) for oy in range(4)
        ]
        rhs = (wa, wb)[kind].at[oz[j]]
        a = jnp.concatenate([tok[:, col] for col in cols], axis=1)
        acc[...] += jnp.dot(a, rhs[...].reshape(1024, WIDTH), preferred_element_type=jnp.float32)

    acc[...] = jnp.zeros_like(acc)
    send_raw(0)
    to_z(0, 0, 2)
    to_z(0, 0, 1)
    send_raw(1)
    send_raw(3)
    to_y(0, z, 1)
    send_raw(2)
    to_y(0, z, 0)
    loads[1].wait()
    island_sum(0)
    island_sum(1)
    island_sum(3)
    zz(0, 1, 0)
    zyu(0, 0, 1)
    zyu(0, 0, 0)
    island_sum(2)
    zyd(0, 0, 0)
    exchange(0)
    share(0)
    loads[2].wait()
    own_global(0)
    exchange(1)
    own_global(1)
    g_to_z()
    zyd(0, 0, 1)
    exchange(3)
    g_to_y(z)
    share(3)
    zyu(0, 1, 0)
    to_z(0, 0, 3)
    zyd(0, 1, 0)
    zzg(2)
    exchange(2)
    zzg(1)
    share(2)
    gf(0)
    zzg(3)
    own3 = own(3)
    to_z(1, 1, 1)
    to_y(1, z, 1)
    share(1)
    gf(2)
    to_z(1, 1, 2)
    zz(0, 2, 0)
    to_z(1, 1, 3)
    xg(0)
    own2 = own(2)
    to_y(1, z, 0)
    gf(3)
    zz(1, 2, 1)
    onward(y, z, has_up, has_dn)
    zz(0, 3, 0)
    xg(2)
    zyd(1, 0, 1)
    to_z(1, 0, 1)
    gf(1)
    zy_far(0, 0, YP)
    onward(y_dn, z, has_up, has_dn)
    to_z(1, 0, 2)
    xf(0)
    own1 = own(1)
    xg(3)
    zyu(1, 0, 1)
    to_z(1, 0, 3)
    own0 = own(0)
    zyd(1, 0, 0)
    onward(y_up, z, has_up, has_dn)
    zyu(1, 0, 0)
    zz(1, 3, 1)
    zz(1, 1, 0)
    place(1, *own1)
    onward(y_far, z, has_up, has_dn)
    blend(0)
    zz(1, 2, 0)
    xg(1)
    finish(2, 0)
    zyu(0, 2, 0)
    place(0, *own0)
    place(3, *own3)
    finish(0, 2)
    zyd(0, 2, 0)
    zz(1, 1, 1)
    yz(2, y)
    finish(0, 0)
    loads[3].wait()
    multiply(0, 0)
    xf(2)
    zyu(1, 2, 1)
    zz(1, 3, 0)
    yz(2, y_dn)
    xf(3)
    finish(1, 0)
    zyd(1, 2, 1)
    yz(1, y_dn)
    yz(1, y)
    finish(0, 3)
    zyu(1, 2, 0)
    zyd(1, 2, 0)
    finish(0, 1)
    finish(2, 1)
    zyu(1, 1, 0)
    yz(2, y_up)
    zyd(0, 3, 0)
    zyu(1, 3, 1)
    zyd(1, 3, 1)
    zyu(0, 3, 0)
    zyd(1, 1, 0)
    yz(1, y_far)
    finish(3, 0)
    finish(2, 3)
    place(2, *own2)
    yz(1, y_up)
    yz(2, y_far)
    for out in outs:
        out.start()
    xf(1)
    blend(2)
    yz(3, y_dn)
    zyu(1, 1, 1)
    multiply(1, 0)
    zyd(1, 3, 0)
    yz(3, y)
    zyd(1, 1, 1)
    finish(3, 3)
    zyu(1, 3, 0)
    multiply(0, 2)
    yz(3, y_far)
    finish(1, 1)
    finish(1, 3)
    finish(2, 2)
    finish(3, 1)
    blend(1)
    yz(3, y_up)
    blend(3)
    multiply(1, 2)
    finish(3, 2)
    finish(1, 2)
    multiply(0, 1)
    multiply(0, 3)
    multiply(1, 1)
    multiply(1, 3)
    keys_v[...] = (acc[...] * (1.0 / math.sqrt(D))).astype(jnp.bfloat16)
    last = pltpu.make_async_copy(keys_v, keys, out_sem.at[2])
    last.start()

    for k in range(CHUNKS):
        s_copy(k).wait_send()
        for d in range(3):
            raw_copy(k, d).wait_send()
            d_copy(k, d).wait_send()

    flat = wb.reshape(32 * HALF * G, WIDTH)

    def sent(t, groups):
        ref = flat.at[pl.ds(0, groups * G)]
        remote(ref, ref, send_sem.at[t], g_rs.at[0], dev_sib).wait_send()

    def size(kind, p, h=None):
        return pieces[kind][p][1] if h is None else parts[kind][p][h][1]

    zfirst = ((0, ZP), (1, 0), (1, 1))
    for h in range(2):
        sent(h, 4 * sum(size(*kp) + size(*kp, h) for kp in zfirst) + size(0, YP) + size(0, YP, h))
    sent(2, 3 * sum(size(*kp) for kp in zfirst))
    for at_z in range(3):
        @pl.when(z == at_z)
        def _(at_z=at_z):
            sent(3, (at_z + 1) * 4 * size(0, YP))

        @pl.when(z == 3 - at_z)
        def _(at_z=at_z):
            sent(4, (at_z + 1) * 4 * size(0, YP))
    sent(5, 3 * 2 + 4 * (2 * 2 + 2))
    sent(6, 4 * (2 * 8 + 2 * 4))
    sent(7, 2 * 4 * 4 * HALF)
    for out in outs:
        out.wait()
    last.wait()


def fused(current, anchor, momentum, tokens, fragment):
    bf, f32 = jnp.bfloat16, jnp.float32
    dma = pltpu.SemaphoreType.DMA
    return pl.pallas_call(
        kernel,
        out_shape=(
            jax.ShapeDtypeStruct((512, WIDTH), bf),
            jax.ShapeDtypeStruct((1, 4, ROWS, WIDTH), bf),
            jax.ShapeDtypeStruct((4, ROWS, WIDTH), f32),
        ),
        in_specs=[pl.BlockSpec(memory_space=pltpu.SMEM)] + [pl.BlockSpec(memory_space=pltpu.HBM)] * 4,
        out_specs=tuple([pl.BlockSpec(memory_space=pl.ANY)] * 3),
        scratch_shapes=[
            pltpu.VMEM((4, ROWS, WIDTH), bf),
            pltpu.VMEM((4, ROWS, WIDTH), bf),
            pltpu.VMEM((4, ROWS, WIDTH), f32),
            pltpu.VMEM((512, D), bf),
            pltpu.VMEM((4, 4, HALF, G, WIDTH), bf),
            pltpu.VMEM((4, 2, 4, HALF, G, WIDTH), bf),
            pltpu.VMEM((4, 2, 4, HALF, G, WIDTH), bf),
            pltpu.VMEM((4, 4, 4, 2, G, WIDTH), bf),
            pltpu.VMEM((16, G, WIDTH), bf),
            pltpu.VMEM((3, CHUNKS, G, WIDTH), bf),
            pltpu.VMEM((CHUNKS, G, WIDTH), bf),
            pltpu.VMEM((CHUNKS, G, WIDTH), bf),
            pltpu.VMEM((16, G, WIDTH), f32),
            pltpu.VMEM((512, WIDTH), bf),
            pltpu.VMEM((512, WIDTH), f32),
            dma((4,)), dma((3,)),
            dma((3, CHUNKS)), dma((3, CHUNKS)), dma((CHUNKS,)), dma((CHUNKS,)),
            dma((3, CHUNKS)), dma((3, CHUNKS)),
            dma((8,)), dma((16, 2, 2)), dma((16, 2, 2)), dma((16,)), dma((4, 2)),
            dma((4, 2)), dma((4, 2)), dma((4,)), dma((4, 4)),
        ],
        compiler_params=pltpu.CompilerParams(
            collective_id=0, has_side_effects=True, vmem_limit_bytes=VMEM
        ),
    )(fragment, current, anchor, momentum, tokens)


def place_kernel(cur_in, mom_in, keys_in, cur, mom, keys):
    cur[...] = cur_in[...]
    mom[...] = mom_in[...]
    keys[...] = keys_in[...]


def local(current, anchor, momentum, tokens, fragment):
    keys, new_current, new_momentum = fused(current, anchor, momentum, tokens, fragment)
    shapes = [jax.ShapeDtypeStruct(a.shape, a.dtype) for a in (new_current, new_momentum, keys)]
    specs = [
        pl.BlockSpec((1, 4, ROWS // 2, WIDTH), lambda i: (0, 0, i, 0)),
        pl.BlockSpec((4, ROWS // 2, WIDTH), lambda i: (0, i, 0)),
        pl.BlockSpec((ROWS, WIDTH), lambda i: (i, 0)),
    ]
    return pl.pallas_call(
        place_kernel,
        out_shape=tuple(shapes),
        grid=(2,),
        in_specs=specs,
        out_specs=tuple(specs),
        compiler_params=pltpu.CompilerParams(vmem_limit_bytes=VMEM),
    )(new_current, new_momentum, keys)


def solution(mesh):
    placed = (
        P("island", None, "fsdp", None),
        P(None, "fsdp", None),
        P(None, "fsdp", None),
        P(("island", "fsdp"), None),
        P(),
    )
    return jax.shard_map(
        local,
        mesh=mesh,
        in_specs=placed,
        out_specs=(
            P("island", None, "fsdp", None),
            P(None, "fsdp", None),
            P(("island", "fsdp"), None),
        ),
        check_vma=False,
    )
```

```python
import math

import jax
import jax.numpy as jnp
from jax import lax
from jax.experimental import pallas as pl
from jax.experimental.pallas import tpu as pltpu
from jax.sharding import PartitionSpec as P

D = 8192
WIDTH = 512
ROWS = 256
G = 16
CHUNKS = 4
MESH = pl.DeviceIdType.MESH
VMEM = 54 * 2**20

outer_momentum = 0.9
outer_rate = 0.7
blend_local = 0.5

HALF = 8
A_PIECES, A_PARTS = ((0, 2), (2, 3), (5, 3)), (((0, 1), (1, 1)), ((2, 2), (4, 1)), ((5, 1), (6, 2)))
B_PIECES, B_PARTS = ((0, 4), (4, 4)), (((0, 2), (2, 2)), ((4, 2), (6, 2)))
YP = 2


def kernel(frag, cur_hbm, anc_hbm, mom_hbm, tok_hbm,
           keys, cur_out, mom_out,
           cur4, anc4, mom4, tok, ra, wa, wb, gb, cur, raw, s_out, s_in, drift, keys_v, acc,
           load_sem, out_sem, raw_ss, raw_rs, s_ss, s_rs, d_ss, d_rs,
           send_sem, a_rs, b_rs, g_rs, gh_rs, x_rs, xh_rs, sib_rs, sibb_rs):
    island = lax.axis_index("island")
    fsdp = lax.axis_index("fsdp")
    zh, x = island // 4, island % 4
    y, z, c = fsdp // 8, (fsdp // 2) % 4, fsdp % 2

    def at(zh_, x_, y_, z_, c_):
        return (zh_ * 4 + x_, y_ * 8 + z_ * 2 + c_)

    low = z < 2
    zm = jnp.where(low, z, 3 - z)

    def zo(j):
        if j == 0:
            return z
        m = j if j > 1 else jnp.where(zm == 0, 1, 0)
        return jnp.where(low, m, 3 - m)

    oz = [zo(j) for j in range(4)]
    y_up, y_dn, y_far = (y + 1) % 4, (y + 3) % 4, (y + 2) % 4
    has_up, has_dn = z < 3, z > 0
    z_up, z_dn = jnp.minimum(z + 1, 3), jnp.maximum(z - 1, 0)
    dev_yu, dev_yd = at(zh, x, y_up, z, c), at(zh, x, y_dn, z, c)
    dev_zu, dev_zd = at(zh, x, y, z_up, c), at(zh, x, y, z_dn, c)
    dev_z = [None] + [at(zh, x, y, oz[j], c) for j in (1, 2, 3)]
    dev_sib = at(zh, x, y, z, 1 - c)
    dev_far = at(1 - zh, x, y, z, c)
    dev_x = [at(zh, (x + d) % 4, y, z, c) for d in (1, 2, 3)]

    loads = [
        pltpu.make_async_copy(cur_hbm.at[0], cur4, load_sem.at[0]),
        pltpu.make_async_copy(anc_hbm, anc4, load_sem.at[1]),
        pltpu.make_async_copy(mom_hbm, mom4, load_sem.at[2]),
        pltpu.make_async_copy(tok_hbm, tok, load_sem.at[3]),
    ]
    for load in loads:
        load.start()

    barrier = pltpu.get_barrier_semaphore()
    peers = (*dev_x, dev_far, dev_yu, dev_yd, *dev_z[1:], dev_sib)
    for dev in peers:
        pl.semaphore_signal(barrier, inc=1, device_id=dev, device_id_type=MESH)

    fr = frag[0]
    loads[0].wait()
    whole = cur4[fr].reshape(16, G, WIDTH)
    cur[...] = whole
    ra[z, y] = whole[:HALF]
    pl.semaphore_wait(barrier, len(peers))

    def remote(src, dst, ss, rs, dev):
        return pltpu.make_async_remote_copy(
            src_ref=src, dst_ref=dst, send_sem=ss, recv_sem=rs,
            device_id=dev, device_id_type=MESH,
        )

    def raw_copy(k, d):
        to = (x + d + 1) % 4
        return remote(cur.at[4 * k + to], raw.at[d, k], raw_ss.at[d, k], raw_rs.at[d, k], dev_x[d])

    def send_raw(k):
        for d in range(3):
            raw_copy(k, d).start()

    def s_copy(k):
        return remote(s_out.at[k], s_in.at[k], s_ss.at[k], s_rs.at[k], dev_far)

    def d_copy(k, d):
        mine = 4 * k + x
        return remote(drift.at[mine], drift.at[mine], d_ss.at[d, k], d_rs.at[d, k], dev_x[d])

    def d_wait(k, d):
        theirs = 4 * k + (x + 3 - d) % 4
        remote(drift.at[theirs], drift.at[theirs], d_ss.at[d, k], d_rs.at[d, k], dev_x[d]).wait_recv()

    def island_sum(k):
        for d in range(3):
            raw_copy(k, d).wait_recv()
        mine = 4 * k + x
        anc = anc4[fr, pl.ds(pl.multiple_of(mine * G, G), G), :].astype(jnp.float32)
        total = cur[mine].astype(jnp.float32) - anc
        for d in range(3):
            total += raw[d, k].astype(jnp.float32) - anc
        s_out[k] = total.astype(jnp.bfloat16)
        s_copy(k).start()

    def step(anc, mom, mean):
        nxt = outer_momentum * mom + mean
        return nxt, anc + outer_rate * (outer_momentum * nxt + mean)

    def exchange(k):
        s_copy(k).wait_recv()
        both = s_out[k].astype(jnp.float32) + s_in[k].astype(jnp.float32)
        drift[4 * k + x] = both * 0.125

    def share(k):
        for d in range(3):
            d_copy(k, d).start()

    def own_global(k):
        rows = pl.ds(pl.multiple_of((4 * k + x) * G, G), G)
        _, glob = step(anc4[fr, rows, :].astype(jnp.float32), mom4[fr, rows, :], drift[4 * k + x])
        gb[z, x, y, k] = glob.astype(jnp.bfloat16)

    def own(k):
        for d in range(3):
            d_wait(k, d)
        rows = pl.ds(64 * k, 64)
        mean = drift[4 * k:4 * k + 4].reshape(64, WIDTH)
        nxt, glob = step(anc4[fr, rows, :].astype(jnp.float32), mom4[fr, rows, :], mean)
        local = cur[4 * k:4 * k + 4].reshape(64, WIDTH).astype(jnp.float32)
        new = (blend_local * local + (1.0 - blend_local) * glob).astype(jnp.bfloat16)
        if k >= 2:
            wb[z, c, y, 4 * k - 8:4 * k - 4] = new.reshape(4, G, WIDTH)
        return nxt, new

    def place(k, nxt, new):
        rows = pl.ds(64 * k, 64)
        for i in range(4):
            mom4[i, rows, :] = jnp.where(fr == i, nxt, mom4[i, rows, :])
            cur4[i, rows, :] = jnp.where(fr == i, new, cur4[i, rows, :])

    outs = [
        pltpu.make_async_copy(cur4, cur_out.at[0], out_sem.at[0]),
        pltpu.make_async_copy(mom4, mom_out, out_sem.at[1]),
    ]

    def block(kind, oy, ozj, span):
        if kind == 0:
            return ra.at[ozj, oy, pl.ds(*span)]
        return wb.at[ozj, c, oy, pl.ds(*span)]

    pieces, parts, arrived = (A_PIECES, B_PIECES), (A_PARTS, B_PARTS), (a_rs, b_rs)

    def go(t, dev, kind, oy, ozj, p, h, span):
        ref = block(kind, oy, ozj, span)
        return remote(ref, ref, send_sem.at[t], arrived[kind].at[ozj * 4 + oy, p, h], dev)

    def arrive(kind, oy, ozj, p, h, span):
        go(0, dev_yu, kind, oy, ozj, p, h, span).wait_recv()

    def to_y(kind, ozj, p):
        go(0, dev_yu, kind, y, ozj, p, 0, pieces[kind][p]).start()
        go(1, dev_yd, kind, y, ozj, p, 0, pieces[kind][p]).start()

    def to_z(kind, p, j):
        go(2, dev_z[j], kind, y, z, p, 0, pieces[kind][p]).start()

    def zz(kind, j, p):
        arrive(kind, y, oz[j], p, 0, pieces[kind][p])
        to_y(kind, oz[j], p)

    def zyd(kind, j, p):
        arrive(kind, y_dn, oz[j], p, 0, pieces[kind][p])
        go(0, dev_yu, kind, y_dn, oz[j], p, 0, parts[kind][p][0]).start()

    def zyu(kind, j, p):
        arrive(kind, y_up, oz[j], p, 0, pieces[kind][p])
        go(1, dev_yd, kind, y_up, oz[j], p, 1, parts[kind][p][1]).start()

    def zy_far(kind, j, p):
        for h in range(2):
            arrive(kind, y_far, oz[j], p, h, parts[kind][p][h])

    def onward(oy, ozj, up, dn):
        @pl.when(up)
        def _():
            go(3, dev_zu, 0, oy, ozj, YP, 0, A_PIECES[YP]).start()

        @pl.when(dn)
        def _():
            go(4, dev_zd, 0, oy, ozj, YP, 0, A_PIECES[YP]).start()

    def yz(j, oy):
        arrive(0, oy, oz[j], YP, 0, A_PIECES[YP])
        onward(oy, oz[j], (oz[j] < z) & has_up, (oz[j] > z) & has_dn)

    def g_copy(oy, ozj, dev):
        ref = gb.at[ozj, x, oy]
        return remote(ref, ref, send_sem.at[5], g_rs.at[ozj * 4 + oy], dev)

    def g_part(oy, ozj, k, dev):
        ref = gb.at[ozj, x, oy, k]
        return remote(ref, ref, send_sem.at[5], gh_rs.at[ozj, k], dev)

    def g_to_y(ozj):
        g_copy(y, ozj, dev_yu).start()
        g_copy(y, ozj, dev_yd).start()

    def g_to_z():
        for dev in dev_z[1:]:
            g_copy(y, z, dev).start()

    def zzg(j):
        g_copy(y, oz[j], dev_yu).wait_recv()
        g_to_y(oz[j])

    def gf(j):
        g_copy(y_dn, oz[j], dev_yu).wait_recv()
        g_part(y_dn, oz[j], 0, dev_yu).start()
        g_copy(y_up, oz[j], dev_yu).wait_recv()
        g_part(y_up, oz[j], 1, dev_yd).start()

    def x_copy(j, d, slot, dev):
        ref = gb.at[oz[j], slot]
        return remote(ref, ref, send_sem.at[6], x_rs.at[oz[j], d], dev)

    def x_part(j, d, slot, dev):
        ref = gb.at[oz[j], slot, pl.ds(2 * d, 2)]
        return remote(ref, ref, send_sem.at[6], xh_rs.at[oz[j], d], dev)

    x_up, x_dn, x_far = (x + 1) % 4, (x + 3) % 4, (x + 2) % 4

    def xg(j):
        for k in range(2):
            g_part(y_far, oz[j], k, dev_yu).wait_recv()
        x_copy(j, 0, x, dev_x[0]).start()
        x_copy(j, 1, x, dev_x[2]).start()

    def xf(j):
        x_copy(j, 0, x_dn, dev_x[0]).wait_recv()
        x_part(j, 0, x_dn, dev_x[0]).start()
        x_copy(j, 1, x_up, dev_x[0]).wait_recv()
        x_part(j, 1, x_up, dev_x[2]).start()

    def sib_a(j):
        ref = wa.at[oz[j], c]
        return remote(ref, ref, send_sem.at[7], sib_rs.at[oz[j]], dev_sib)

    def sib_b(j, oy, core):
        ref = wb.at[oz[j], core, oy]
        return remote(ref, ref, send_sem.at[7], sibb_rs.at[oz[j], oy], dev_sib)

    def sib_wait(kind, j):
        if kind == 0:
            ref = wa.at[oz[j], 1 - c]
            remote(ref, ref, send_sem.at[7], sib_rs.at[oz[j]], dev_sib).wait_recv()
        else:
            for oy in range(4):
                sib_b(j, oy, 1 - c).wait_recv()

    def blend(j):
        for p in range(YP):
            zy_far(0, j, p)
        for d in range(2):
            x_part(j, d, x_far, dev_x[0]).wait_recv()

        def one(oy, _):
            for k in range(2):
                for q in range(4):
                    mix = blend_local * ra[oz[j], oy, 4 * k + q].astype(jnp.float32)
                    mix += (1.0 - blend_local) * gb[oz[j], q, oy, k].astype(jnp.float32)
                    wa[oz[j], c, oy, 4 * k + q] = mix.astype(jnp.bfloat16)
            return 0

        lax.fori_loop(0, 4, one, 0)
        sib_a(j).start()

    def finish(j, r):
        oy = (y, y_up, y_far, y_dn)[r]
        if r == 2:
            for p in range(2):
                zy_far(1, j, p)
        sib_b(j, oy, c).start()

    def multiply(kind, j):
        sib_wait(kind, j)

        cols = [
            pl.ds(pl.multiple_of((oy * 8 + oz[j] * 2 + core) * ROWS + kind * 128, 128), 128)
            for core in range(2) for oy in range(4)
        ]
        rhs = (wa, wb)[kind].at[oz[j]]
        a = jnp.concatenate([tok[:, col] for col in cols], axis=1)
        acc[...] += jnp.dot(a, rhs[...].reshape(1024, WIDTH), preferred_element_type=jnp.float32)

    acc[...] = jnp.zeros_like(acc)
    send_raw(0)
    to_y(0, z, 2)
    to_z(0, 1, 1)
    to_z(0, 1, 3)
    send_raw(1)
    to_y(0, z, 1)
    send_raw(2)
    to_z(0, 0, 1)
    to_z(0, 1, 2)
    send_raw(3)
    to_y(0, z, 0)
    loads[1].wait()
    island_sum(0)
    zz(0, 1, 1)
    island_sum(1)
    zyd(0, 0, 2)
    island_sum(2)
    zz(0, 2, 1)
    island_sum(3)
    zyu(0, 0, 2)
    zz(0, 1, 0)
    zyd(0, 0, 0)
    zz(0, 3, 1)
    zyd(0, 1, 1)
    zyd(0, 0, 1)
    to_z(0, 0, 2)
    exchange(0)
    zyu(0, 0, 0)
    loads[2].wait()
    own_global(0)
    exchange(1)
    own_global(1)
    g_to_z()
    onward(y, z, has_up, has_dn)
    zy_far(0, 0, YP)
    exchange(2)
    g_to_y(z)
    zyd(0, 1, 0)
    to_z(0, 0, 3)
    zyd(0, 2, 1)
    share(2)
    exchange(3)
    zyu(0, 0, 1)
    zyu(0, 2, 1)
    zyu(0, 1, 1)
    share(3)
    share(1)
    zyd(0, 3, 1)
    zyu(0, 1, 0)
    onward(y_up, z, has_up, has_dn)
    share(0)
    zzg(2)
    gf(0)
    zzg(1)
    zzg(3)
    own2 = own(2)
    to_y(1, z, 0)
    to_z(1, 0, 2)
    gf(2)
    zyu(0, 3, 1)
    xg(0)
    to_z(1, 0, 1)
    own3 = own(3)
    to_z(1, 0, 3)
    place(3, *own3)
    to_y(1, z, 1)
    zz(0, 2, 0)
    zz(0, 3, 0)
    gf(1)
    own1 = own(1)
    to_z(1, 1, 1)
    to_z(1, 1, 2)
    finish(0, 0)
    onward(y_far, z, has_up, has_dn)
    zyu(1, 0, 0)
    xg(2)
    yz(1, y)
    zyd(1, 0, 0)
    gf(3)
    zyd(1, 0, 1)
    zyu(1, 0, 1)
    zz(1, 2, 0)
    xf(0)
    own0 = own(0)
    to_z(1, 1, 3)
    zyd(0, 2, 0)
    xg(1)
    zz(1, 3, 0)
    zz(1, 1, 0)
    finish(0, 3)
    onward(y_dn, z, has_up, has_dn)
    yz(2, y_up)
    zz(1, 1, 1)
    finish(0, 1)
    xg(3)
    yz(2, y)
    zyu(0, 2, 0)
    blend(0)
    finish(0, 2)
    yz(1, y_far)
    zyu(1, 2, 0)
    zz(1, 3, 1)
    finish(1, 0)
    loads[3].wait()
    multiply(0, 0)
    xf(1)
    zz(1, 2, 1)
    zyd(1, 1, 0)
    finish(3, 0)
    zyd(0, 3, 0)
    zyu(1, 1, 0)
    place(0, *own0)
    xf(2)
    yz(2, y_far)
    multiply(1, 0)
    place(1, *own1)
    zyu(1, 1, 1)
    zyd(1, 3, 0)
    yz(3, y)
    zyu(0, 3, 0)
    finish(1, 1)
    yz(1, y_dn)
    zyd(1, 1, 1)
    xf(3)
    zyu(1, 3, 0)
    place(2, *own2)
    zyd(1, 3, 1)
    yz(1, y_up)
    for out in outs:
        out.start()
    zyd(1, 2, 0)
    finish(2, 0)
    yz(2, y_dn)
    blend(1)
    zyu(1, 3, 1)
    finish(1, 3)
    zyd(1, 2, 1)
    yz(3, y_far)
    finish(3, 3)
    finish(2, 3)
    finish(3, 1)
    zyu(1, 2, 1)
    blend(2)
    yz(3, y_dn)
    finish(2, 1)
    multiply(0, 1)
    finish(1, 2)
    yz(3, y_up)
    blend(3)
    finish(3, 2)
    multiply(0, 2)
    finish(2, 2)
    multiply(1, 1)
    multiply(1, 3)
    multiply(0, 3)
    multiply(1, 2)
    keys_v[...] = (acc[...] * (1.0 / math.sqrt(D))).astype(jnp.bfloat16)
    last = pltpu.make_async_copy(keys_v, keys, out_sem.at[2])
    last.start()

    for k in range(CHUNKS):
        s_copy(k).wait_send()
        for d in range(3):
            raw_copy(k, d).wait_send()
            d_copy(k, d).wait_send()

    flat = wb.reshape(32 * HALF * G, WIDTH)

    def sent(t, groups):
        ref = flat.at[pl.ds(0, groups * G)]
        remote(ref, ref, send_sem.at[t], g_rs.at[0], dev_sib).wait_send()

    def size(kind, p, h=None):
        return pieces[kind][p][1] if h is None else parts[kind][p][h][1]

    zfirst = ((0, 0), (0, 1), (1, 0), (1, 1))
    for h in range(2):
        sent(h, 4 * sum(size(*kp) + size(*kp, h) for kp in zfirst) + size(0, YP) + size(0, YP, h))
    sent(2, 3 * sum(size(*kp) for kp in zfirst))
    for at_z in range(3):
        @pl.when(z == at_z)
        def _(at_z=at_z):
            sent(3, (at_z + 1) * 4 * size(0, YP))

        @pl.when(z == 3 - at_z)
        def _(at_z=at_z):
            sent(4, (at_z + 1) * 4 * size(0, YP))
    sent(5, 3 * 2 + 4 * (2 * 2 + 2))
    sent(6, 4 * (2 * 8 + 2 * 4))
    sent(7, 2 * 4 * 4 * HALF)
    for out in outs:
        out.wait()
    last.wait()


def fused(current, anchor, momentum, tokens, fragment):
    bf, f32 = jnp.bfloat16, jnp.float32
    dma = pltpu.SemaphoreType.DMA
    return pl.pallas_call(
        kernel,
        out_shape=(
            pltpu.VMEM((512, WIDTH), bf),
            pltpu.VMEM((1, 4, ROWS, WIDTH), bf),
            pltpu.VMEM((4, ROWS, WIDTH), f32),
        ),
        in_specs=[pl.BlockSpec(memory_space=pltpu.SMEM)] + [pl.BlockSpec(memory_space=pltpu.HBM)] * 4,
        out_specs=tuple([pl.BlockSpec(memory_space=pl.ANY)] * 3),
        scratch_shapes=[
            pltpu.VMEM((4, ROWS, WIDTH), bf),
            pltpu.VMEM((4, ROWS, WIDTH), bf),
            pltpu.VMEM((4, ROWS, WIDTH), f32),
            pltpu.VMEM((512, D), bf),
            pltpu.VMEM((4, 4, HALF, G, WIDTH), bf),
            pltpu.VMEM((4, 2, 4, HALF, G, WIDTH), bf),
            pltpu.VMEM((4, 2, 4, HALF, G, WIDTH), bf),
            pltpu.VMEM((4, 4, 4, 2, G, WIDTH), bf),
            pltpu.VMEM((16, G, WIDTH), bf),
            pltpu.VMEM((3, CHUNKS, G, WIDTH), bf),
            pltpu.VMEM((CHUNKS, G, WIDTH), bf),
            pltpu.VMEM((CHUNKS, G, WIDTH), bf),
            pltpu.VMEM((16, G, WIDTH), f32),
            pltpu.VMEM((512, WIDTH), bf),
            pltpu.VMEM((512, WIDTH), f32),
            dma((4,)), dma((3,)),
            dma((3, CHUNKS)), dma((3, CHUNKS)), dma((CHUNKS,)), dma((CHUNKS,)),
            dma((3, CHUNKS)), dma((3, CHUNKS)),
            dma((8,)), dma((16, 3, 2)), dma((16, 2, 2)), dma((16,)), dma((4, 2)),
            dma((4, 2)), dma((4, 2)), dma((4,)), dma((4, 4)),
        ],
        compiler_params=pltpu.CompilerParams(
            collective_id=0, has_side_effects=True, vmem_limit_bytes=VMEM
        ),
    )(fragment, current, anchor, momentum, tokens)


def place_kernel(cur_in, mom_in, keys_in, cur, mom, keys, sem):
    moves = [(mom_in.at[i], mom.at[i]) for i in range(4)]
    moves += [(cur_in.at[0, pl.ds(2 * i, 2)], cur.at[0, pl.ds(2 * i, 2)]) for i in range(2)]
    moves += [(keys_in, keys)]
    copies = [pltpu.make_async_copy(a, b, sem.at[i]) for i, (a, b) in enumerate(moves)]
    for copy in copies:
        copy.start()
    for copy in copies:
        copy.wait()


def local(current, anchor, momentum, tokens, fragment):
    keys, new_current, new_momentum = fused(current, anchor, momentum, tokens, fragment)
    shapes = [jax.ShapeDtypeStruct(a.shape, a.dtype) for a in (current, momentum, keys)]
    return pl.pallas_call(
        place_kernel,
        out_shape=tuple(shapes),
        in_specs=[pl.BlockSpec(memory_space=pl.ANY)] * 3,
        out_specs=tuple([pl.BlockSpec(memory_space=pl.ANY)] * 3),
        scratch_shapes=[pltpu.SemaphoreType.DMA((7,))],
        compiler_params=pltpu.CompilerParams(vmem_limit_bytes=16 * 2**20),
    )(new_current, new_momentum, keys)


def solution(mesh):
    placed = (
        P("island", None, "fsdp", None),
        P(None, "fsdp", None),
        P(None, "fsdp", None),
        P(("island", "fsdp"), None),
        P(),
    )
    return jax.shard_map(
        local,
        mesh=mesh,
        in_specs=placed,
        out_specs=(
            P("island", None, "fsdp", None),
            P(None, "fsdp", None),
            P(("island", "fsdp"), None),
        ),
        check_vma=False,
    )
```

```python
import math

import jax
import jax.numpy as jnp
from jax import lax
from jax.experimental import pallas as pl
from jax.experimental.pallas import tpu as pltpu
from jax.sharding import PartitionSpec as P

D = 8192
WIDTH = 512
ROWS = 256
G = 16
CHUNKS = 4
MESH = pl.DeviceIdType.MESH
VMEM = 54 * 2**20

outer_momentum = 0.9
outer_rate = 0.7
blend_local = 0.5

HALF = 8
A_PIECES, A_PARTS = ((0, 2), (2, 3), (5, 3)), (((0, 1), (1, 1)), ((2, 2), (4, 1)), ((5, 1), (6, 2)))
B_PIECES, B_PARTS = ((0, 4), (4, 4)), (((0, 2), (2, 2)), ((4, 2), (6, 2)))
YP = 2


def kernel(frag, cur_hbm, anc_hbm, mom_hbm, tok_hbm,
           keys, cur_out, mom_out,
           cur4, anc4, mom4, tok, ra, wa, wb, gb, cur, raw, s_out, s_in, drift, acc,
           load_sem, out_sem, raw_ss, raw_rs, s_ss, s_rs, d_ss, d_rs,
           send_sem, a_rs, b_rs, g_rs, gh_rs, x_rs, xh_rs, sib_rs, sibb_rs):
    island = lax.axis_index("island")
    fsdp = lax.axis_index("fsdp")
    zh, x = island // 4, island % 4
    y, z, c = fsdp // 8, (fsdp // 2) % 4, fsdp % 2

    def at(zh_, x_, y_, z_, c_):
        return (zh_ * 4 + x_, y_ * 8 + z_ * 2 + c_)

    low = z < 2
    zm = jnp.where(low, z, 3 - z)

    def zo(j):
        if j == 0:
            return z
        m = j if j > 1 else jnp.where(zm == 0, 1, 0)
        return jnp.where(low, m, 3 - m)

    oz = [zo(j) for j in range(4)]
    y_up, y_dn, y_far = (y + 1) % 4, (y + 3) % 4, (y + 2) % 4
    has_up, has_dn = z < 3, z > 0
    z_up, z_dn = jnp.minimum(z + 1, 3), jnp.maximum(z - 1, 0)
    dev_yu, dev_yd = at(zh, x, y_up, z, c), at(zh, x, y_dn, z, c)
    dev_zu, dev_zd = at(zh, x, y, z_up, c), at(zh, x, y, z_dn, c)
    dev_z = [None] + [at(zh, x, y, oz[j], c) for j in (1, 2, 3)]
    dev_sib = at(zh, x, y, z, 1 - c)
    dev_far = at(1 - zh, x, y, z, c)
    dev_x = [at(zh, (x + d) % 4, y, z, c) for d in (1, 2, 3)]

    loads = [
        pltpu.make_async_copy(cur_hbm.at[0], cur4, load_sem.at[0]),
        pltpu.make_async_copy(anc_hbm, anc4, load_sem.at[1]),
        pltpu.make_async_copy(mom_hbm, mom4, load_sem.at[2]),
        pltpu.make_async_copy(tok_hbm, tok, load_sem.at[3]),
    ]
    for load in loads:
        load.start()

    barrier = pltpu.get_barrier_semaphore()
    peers = (*dev_x, dev_far, dev_yu, dev_yd, *dev_z[1:], dev_sib)
    for dev in peers:
        pl.semaphore_signal(barrier, inc=1, device_id=dev, device_id_type=MESH)

    fr = frag[0]
    loads[0].wait()
    whole = cur4[fr].reshape(16, G, WIDTH)
    cur[...] = whole
    ra[z, y] = whole[:HALF]
    pl.semaphore_wait(barrier, len(peers))

    def remote(src, dst, ss, rs, dev):
        return pltpu.make_async_remote_copy(
            src_ref=src, dst_ref=dst, send_sem=ss, recv_sem=rs,
            device_id=dev, device_id_type=MESH,
        )

    def raw_copy(k, d):
        to = (x + d + 1) % 4
        return remote(cur.at[4 * k + to], raw.at[d, k], raw_ss.at[d, k], raw_rs.at[d, k], dev_x[d])

    def send_raw(k):
        for d in range(3):
            raw_copy(k, d).start()

    def s_copy(k):
        return remote(s_out.at[k], s_in.at[k], s_ss.at[k], s_rs.at[k], dev_far)

    def d_copy(k, d):
        mine = 4 * k + x
        return remote(drift.at[mine], drift.at[mine], d_ss.at[d, k], d_rs.at[d, k], dev_x[d])

    def d_wait(k, d):
        theirs = 4 * k + (x + 3 - d) % 4
        remote(drift.at[theirs], drift.at[theirs], d_ss.at[d, k], d_rs.at[d, k], dev_x[d]).wait_recv()

    def island_sum(k):
        for d in range(3):
            raw_copy(k, d).wait_recv()
        mine = 4 * k + x
        anc = anc4[fr, pl.ds(pl.multiple_of(mine * G, G), G), :].astype(jnp.float32)
        total = cur[mine].astype(jnp.float32) - anc
        for d in range(3):
            total += raw[d, k].astype(jnp.float32) - anc
        s_out[k] = total.astype(jnp.bfloat16)
        s_copy(k).start()

    def step(anc, mom, mean):
        nxt = outer_momentum * mom + mean
        return nxt, anc + outer_rate * (outer_momentum * nxt + mean)

    def exchange(k):
        s_copy(k).wait_recv()
        both = s_out[k].astype(jnp.float32) + s_in[k].astype(jnp.float32)
        drift[4 * k + x] = both * 0.125

    def share(k):
        for d in range(3):
            d_copy(k, d).start()

    def own_global(k):
        rows = pl.ds(pl.multiple_of((4 * k + x) * G, G), G)
        _, glob = step(anc4[fr, rows, :].astype(jnp.float32), mom4[fr, rows, :], drift[4 * k + x])
        gb[z, x, y, k] = glob.astype(jnp.bfloat16)

    def own(k):
        for d in range(3):
            d_wait(k, d)
        rows = pl.ds(64 * k, 64)
        mean = drift[4 * k:4 * k + 4].reshape(64, WIDTH)
        nxt, glob = step(anc4[fr, rows, :].astype(jnp.float32), mom4[fr, rows, :], mean)
        local = cur[4 * k:4 * k + 4].reshape(64, WIDTH).astype(jnp.float32)
        new = (blend_local * local + (1.0 - blend_local) * glob).astype(jnp.bfloat16)
        if k >= 2:
            wb[z, c, y, 4 * k - 8:4 * k - 4] = new.reshape(4, G, WIDTH)
        return nxt, new

    def place(k, nxt, new):
        rows = pl.ds(64 * k, 64)
        for i in range(4):
            mom4[i, rows, :] = jnp.where(fr == i, nxt, mom4[i, rows, :])
            cur4[i, rows, :] = jnp.where(fr == i, new, cur4[i, rows, :])

    outs = [
        pltpu.make_async_copy(cur4, cur_out.at[0], out_sem.at[0]),
        pltpu.make_async_copy(mom4, mom_out, out_sem.at[1]),
    ]

    def block(kind, oy, ozj, span):
        if kind == 0:
            return ra.at[ozj, oy, pl.ds(*span)]
        return wb.at[ozj, c, oy, pl.ds(*span)]

    pieces, parts, arrived = (A_PIECES, B_PIECES), (A_PARTS, B_PARTS), (a_rs, b_rs)

    def go(t, dev, kind, oy, ozj, p, h, span):
        ref = block(kind, oy, ozj, span)
        return remote(ref, ref, send_sem.at[t], arrived[kind].at[ozj * 4 + oy, p, h], dev)

    def arrive(kind, oy, ozj, p, h, span):
        go(0, dev_yu, kind, oy, ozj, p, h, span).wait_recv()

    def to_y(kind, ozj, p):
        go(0, dev_yu, kind, y, ozj, p, 0, pieces[kind][p]).start()
        go(1, dev_yd, kind, y, ozj, p, 0, pieces[kind][p]).start()

    def to_z(kind, p, j):
        go(2, dev_z[j], kind, y, z, p, 0, pieces[kind][p]).start()

    def zz(kind, j, p):
        arrive(kind, y, oz[j], p, 0, pieces[kind][p])
        to_y(kind, oz[j], p)

    def zyd(kind, j, p):
        arrive(kind, y_dn, oz[j], p, 0, pieces[kind][p])
        go(0, dev_yu, kind, y_dn, oz[j], p, 0, parts[kind][p][0]).start()

    def zyu(kind, j, p):
        arrive(kind, y_up, oz[j], p, 0, pieces[kind][p])
        go(1, dev_yd, kind, y_up, oz[j], p, 1, parts[kind][p][1]).start()

    def zy_far(kind, j, p):
        for h in range(2):
            arrive(kind, y_far, oz[j], p, h, parts[kind][p][h])

    def onward(oy, ozj, up, dn):
        @pl.when(up)
        def _():
            go(3, dev_zu, 0, oy, ozj, YP, 0, A_PIECES[YP]).start()

        @pl.when(dn)
        def _():
            go(4, dev_zd, 0, oy, ozj, YP, 0, A_PIECES[YP]).start()

    def yz(j, oy):
        arrive(0, oy, oz[j], YP, 0, A_PIECES[YP])
        onward(oy, oz[j], (oz[j] < z) & has_up, (oz[j] > z) & has_dn)

    def g_copy(oy, ozj, dev):
        ref = gb.at[ozj, x, oy]
        return remote(ref, ref, send_sem.at[5], g_rs.at[ozj * 4 + oy], dev)

    def g_part(oy, ozj, k, dev):
        ref = gb.at[ozj, x, oy, k]
        return remote(ref, ref, send_sem.at[5], gh_rs.at[ozj, k], dev)

    def g_to_y(ozj):
        g_copy(y, ozj, dev_yu).start()
        g_copy(y, ozj, dev_yd).start()

    def g_to_z():
        for dev in dev_z[1:]:
            g_copy(y, z, dev).start()

    def zzg(j):
        g_copy(y, oz[j], dev_yu).wait_recv()
        g_to_y(oz[j])

    def gf(j):
        g_copy(y_dn, oz[j], dev_yu).wait_recv()
        g_part(y_dn, oz[j], 0, dev_yu).start()
        g_copy(y_up, oz[j], dev_yu).wait_recv()
        g_part(y_up, oz[j], 1, dev_yd).start()

    def x_copy(j, d, slot, dev):
        ref = gb.at[oz[j], slot]
        return remote(ref, ref, send_sem.at[6], x_rs.at[oz[j], d], dev)

    def x_part(j, d, slot, dev):
        ref = gb.at[oz[j], slot, pl.ds(2 * d, 2)]
        return remote(ref, ref, send_sem.at[6], xh_rs.at[oz[j], d], dev)

    x_up, x_dn, x_far = (x + 1) % 4, (x + 3) % 4, (x + 2) % 4

    def xg(j):
        for k in range(2):
            g_part(y_far, oz[j], k, dev_yu).wait_recv()
        x_copy(j, 0, x, dev_x[0]).start()
        x_copy(j, 1, x, dev_x[2]).start()

    def xf(j):
        x_copy(j, 0, x_dn, dev_x[0]).wait_recv()
        x_part(j, 0, x_dn, dev_x[0]).start()
        x_copy(j, 1, x_up, dev_x[0]).wait_recv()
        x_part(j, 1, x_up, dev_x[2]).start()

    def sib_a(j):
        ref = wa.at[oz[j], c]
        return remote(ref, ref, send_sem.at[7], sib_rs.at[oz[j]], dev_sib)

    def sib_b(j, oy, core):
        ref = wb.at[oz[j], core, oy]
        return remote(ref, ref, send_sem.at[7], sibb_rs.at[oz[j], oy], dev_sib)

    def sib_wait(kind, j):
        if kind == 0:
            ref = wa.at[oz[j], 1 - c]
            remote(ref, ref, send_sem.at[7], sib_rs.at[oz[j]], dev_sib).wait_recv()
        else:
            for oy in range(4):
                sib_b(j, oy, 1 - c).wait_recv()

    def blend(j):
        for p in range(YP):
            zy_far(0, j, p)
        for d in range(2):
            x_part(j, d, x_far, dev_x[0]).wait_recv()

        def one(oy, _):
            for k in range(2):
                for q in range(4):
                    mix = blend_local * ra[oz[j], oy, 4 * k + q].astype(jnp.float32)
                    mix += (1.0 - blend_local) * gb[oz[j], q, oy, k].astype(jnp.float32)
                    wa[oz[j], c, oy, 4 * k + q] = mix.astype(jnp.bfloat16)
            return 0

        lax.fori_loop(0, 4, one, 0)
        sib_a(j).start()

    def finish(j, r):
        oy = (y, y_up, y_far, y_dn)[r]
        if r == 2:
            for p in range(2):
                zy_far(1, j, p)
        sib_b(j, oy, c).start()

    def multiply(kind, j, last=False):
        sib_wait(kind, j)

        cols = [
            pl.ds(pl.multiple_of((oy * 8 + oz[j] * 2 + core) * ROWS + kind * 128, 128), 128)
            for core in range(2) for oy in range(4)
        ]
        rhs = (wa, wb)[kind].at[oz[j]]
        a = jnp.concatenate([tok[:, col] for col in cols], axis=1)
        total = acc[...] + jnp.dot(a, rhs[...].reshape(1024, WIDTH), preferred_element_type=jnp.float32)
        if last:
            keys[...] = (total * (1.0 / math.sqrt(D))).astype(jnp.bfloat16)
        else:
            acc[...] = total

    def left_early():
        for k in range(CHUNKS):
            s_copy(k).wait_send()
            for d in range(3):
                raw_copy(k, d).wait_send()

    def left_shares():
        for k in range(CHUNKS):
            for d in range(3):
                d_copy(k, d).wait_send()


    acc[...] = jnp.zeros_like(acc)
    send_raw(0)
    to_y(0, z, 2)
    to_z(0, 1, 1)
    to_z(0, 1, 3)
    send_raw(1)
    to_y(0, z, 1)
    send_raw(2)
    to_z(0, 0, 1)
    to_z(0, 1, 2)
    send_raw(3)
    to_y(0, z, 0)
    loads[1].wait()
    island_sum(0)
    zz(0, 1, 1)
    island_sum(1)
    zyd(0, 0, 2)
    island_sum(2)
    zz(0, 2, 1)
    island_sum(3)
    zyu(0, 0, 2)
    zz(0, 1, 0)
    zyd(0, 0, 0)
    zz(0, 3, 1)
    zyd(0, 1, 1)
    zyd(0, 0, 1)
    to_z(0, 0, 2)
    exchange(0)
    zyu(0, 0, 0)
    loads[2].wait()
    own_global(0)
    exchange(1)
    own_global(1)
    g_to_z()
    onward(y, z, has_up, has_dn)
    zy_far(0, 0, YP)
    exchange(2)
    g_to_y(z)
    zyd(0, 1, 0)
    to_z(0, 0, 3)
    zyd(0, 2, 1)
    share(2)
    exchange(3)
    zyu(0, 0, 1)
    zyu(0, 2, 1)
    zyu(0, 1, 1)
    share(3)
    share(1)
    zyd(0, 3, 1)
    zyu(0, 1, 0)
    onward(y_up, z, has_up, has_dn)
    share(0)
    zzg(2)
    gf(0)
    zzg(1)
    zzg(3)
    own2 = own(2)
    to_y(1, z, 0)
    to_z(1, 0, 2)
    gf(2)
    zyu(0, 3, 1)
    xg(0)
    to_z(1, 0, 1)
    own3 = own(3)
    to_z(1, 0, 3)
    place(3, *own3)
    to_y(1, z, 1)
    zz(0, 2, 0)
    zz(0, 3, 0)
    gf(1)
    own1 = own(1)
    to_z(1, 1, 1)
    to_z(1, 1, 2)
    finish(0, 0)
    onward(y_far, z, has_up, has_dn)
    zyu(1, 0, 0)
    xg(2)
    yz(1, y)
    zyd(1, 0, 0)
    gf(3)
    zyd(1, 0, 1)
    zyu(1, 0, 1)
    zz(1, 2, 0)
    xf(0)
    own0 = own(0)
    to_z(1, 1, 3)
    zyd(0, 2, 0)
    xg(1)
    zz(1, 3, 0)
    zz(1, 1, 0)
    finish(0, 3)
    onward(y_dn, z, has_up, has_dn)
    yz(2, y_up)
    zz(1, 1, 1)
    finish(0, 1)
    xg(3)
    yz(2, y)
    zyu(0, 2, 0)
    blend(0)
    finish(0, 2)
    yz(1, y_far)
    zyu(1, 2, 0)
    zz(1, 3, 1)
    finish(1, 0)
    loads[3].wait()
    multiply(0, 0)
    xf(1)
    zz(1, 2, 1)
    zyd(1, 1, 0)
    finish(3, 0)
    zyd(0, 3, 0)
    zyu(1, 1, 0)
    place(0, *own0)
    xf(2)
    yz(2, y_far)
    multiply(1, 0)
    place(1, *own1)
    zyu(1, 1, 1)
    zyd(1, 3, 0)
    yz(3, y)
    zyu(0, 3, 0)
    finish(1, 1)
    yz(1, y_dn)
    zyd(1, 1, 1)
    xf(3)
    zyu(1, 3, 0)
    place(2, *own2)
    zyd(1, 3, 1)
    yz(1, y_up)
    for out in outs:
        out.start()
    zyd(1, 2, 0)
    finish(2, 0)
    yz(2, y_dn)
    blend(1)
    zyu(1, 3, 1)
    finish(1, 3)
    zyd(1, 2, 1)
    yz(3, y_far)
    finish(3, 3)
    finish(2, 3)
    finish(3, 1)
    zyu(1, 2, 1)
    blend(2)
    yz(3, y_dn)
    finish(2, 1)
    multiply(0, 1)
    finish(1, 2)
    yz(3, y_up)
    blend(3)
    finish(3, 2)
    multiply(0, 2)
    finish(2, 2)
    left_early()
    multiply(1, 1)
    left_shares()
    multiply(1, 3)
    multiply(0, 3)
    multiply(1, 2, True)

    flat = wb.reshape(32 * HALF * G, WIDTH)

    def sent(t, groups):
        ref = flat.at[pl.ds(0, groups * G)]
        remote(ref, ref, send_sem.at[t], g_rs.at[0], dev_sib).wait_send()

    def size(kind, p, h=None):
        return pieces[kind][p][1] if h is None else parts[kind][p][h][1]

    zfirst = ((0, 0), (0, 1), (1, 0), (1, 1))
    for h in range(2):
        sent(h, 4 * sum(size(*kp) + size(*kp, h) for kp in zfirst) + size(0, YP) + size(0, YP, h))
    sent(2, 3 * sum(size(*kp) for kp in zfirst))
    for at_z in range(3):
        @pl.when(z == at_z)
        def _(at_z=at_z):
            sent(3, (at_z + 1) * 4 * size(0, YP))

        @pl.when(z == 3 - at_z)
        def _(at_z=at_z):
            sent(4, (at_z + 1) * 4 * size(0, YP))
    sent(5, 3 * 2 + 4 * (2 * 2 + 2))
    sent(6, 4 * (2 * 8 + 2 * 4))
    sent(7, 2 * 4 * 4 * HALF)
    for out in outs:
        out.wait()


def fused(current, anchor, momentum, tokens, fragment):
    bf, f32 = jnp.bfloat16, jnp.float32
    dma = pltpu.SemaphoreType.DMA
    return pl.pallas_call(
        kernel,
        out_shape=(
            pltpu.VMEM((512, WIDTH), bf),
            pltpu.VMEM((1, 4, ROWS, WIDTH), bf),
            pltpu.VMEM((4, ROWS, WIDTH), f32),
        ),
        in_specs=[pl.BlockSpec(memory_space=pltpu.SMEM)] + [pl.BlockSpec(memory_space=pltpu.HBM)] * 4,
        out_specs=(pl.BlockSpec(memory_space=pltpu.VMEM),) + tuple([pl.BlockSpec(memory_space=pl.ANY)] * 2),
        scratch_shapes=[
            pltpu.VMEM((4, ROWS, WIDTH), bf),
            pltpu.VMEM((4, ROWS, WIDTH), bf),
            pltpu.VMEM((4, ROWS, WIDTH), f32),
            pltpu.VMEM((512, D), bf),
            pltpu.VMEM((4, 4, HALF, G, WIDTH), bf),
            pltpu.VMEM((4, 2, 4, HALF, G, WIDTH), bf),
            pltpu.VMEM((4, 2, 4, HALF, G, WIDTH), bf),
            pltpu.VMEM((4, 4, 4, 2, G, WIDTH), bf),
            pltpu.VMEM((16, G, WIDTH), bf),
            pltpu.VMEM((3, CHUNKS, G, WIDTH), bf),
            pltpu.VMEM((CHUNKS, G, WIDTH), bf),
            pltpu.VMEM((CHUNKS, G, WIDTH), bf),
            pltpu.VMEM((16, G, WIDTH), f32),
            pltpu.VMEM((512, WIDTH), f32),
            dma((4,)), dma((2,)),
            dma((3, CHUNKS)), dma((3, CHUNKS)), dma((CHUNKS,)), dma((CHUNKS,)),
            dma((3, CHUNKS)), dma((3, CHUNKS)),
            dma((8,)), dma((16, 3, 2)), dma((16, 2, 2)), dma((16,)), dma((4, 2)),
            dma((4, 2)), dma((4, 2)), dma((4,)), dma((4, 4)),
        ],
        compiler_params=pltpu.CompilerParams(
            collective_id=0, has_side_effects=True, vmem_limit_bytes=VMEM
        ),
    )(fragment, current, anchor, momentum, tokens)


def place_kernel(cur_in, mom_in, keys_in, cur, mom, keys, sem):
    moves = ((mom_in, mom), (cur_in, cur), (keys_in, keys))
    copies = [pltpu.make_async_copy(a, b, sem.at[i]) for i, (a, b) in enumerate(moves)]
    for copy in copies:
        copy.start()
    for copy in copies:
        copy.wait()


def local(current, anchor, momentum, tokens, fragment):
    keys, new_current, new_momentum = fused(current, anchor, momentum, tokens, fragment)
    shapes = [jax.ShapeDtypeStruct(a.shape, a.dtype) for a in (current, momentum, keys)]
    return pl.pallas_call(
        place_kernel,
        out_shape=tuple(shapes),
        in_specs=[pl.BlockSpec(memory_space=pl.ANY)] * 3,
        out_specs=tuple([pl.BlockSpec(memory_space=pl.ANY)] * 3),
        scratch_shapes=[pltpu.SemaphoreType.DMA((3,))],
        compiler_params=pltpu.CompilerParams(vmem_limit_bytes=16 * 2**20),
    )(new_current, new_momentum, keys)


def solution(mesh):
    placed = (
        P("island", None, "fsdp", None),
        P(None, "fsdp", None),
        P(None, "fsdp", None),
        P(("island", "fsdp"), None),
        P(),
    )
    return jax.shard_map(
        local,
        mesh=mesh,
        in_specs=placed,
        out_specs=(
            P("island", None, "fsdp", None),
            P(None, "fsdp", None),
            P(("island", "fsdp"), None),
        ),
        check_vma=False,
    )
```
